32 devices in a mesh: sector: 4 (over y, core), term: 8 (over z, x).
Axes of the slice: x: 2, y: 2, z: 4, core: 2. Of those that a mesh axis runs over, the one named last changes fastest.
Arguments:
- trial: float32 [8, 512, 512], P('sector', 'term'), may hold values from -6 to 6
- precond: float32 [8, 512, 512], P('sector', 'term'), may hold values from 2 to 16
- sector_dims: int32 [8], P('sector'), may hold values from 128 to 512
- left_ops: float32 [256, 512, 512], P(('sector', 'term')), may hold values from -0.25 to 0.25
- right_ops: float32 [256, 512, 512], P(('sector', 'term')), may hold values from -0.25 to 0.25
- task_source: int32 [256], P(('sector', 'term')), may hold values from 0 to 1
- task_target: int32 [256], P(('sector', 'term')), may hold values from 0 to 1
- task_count: int32 [32], P(('sector', 'term')), may hold values from 1 to 7, as said below
Outputs:
- trial_out: float32 [8, 512, 512], P('sector', 'term')
- ritz: float32 [3], replicated
The draws below stay inside these ranges and needn't reach their ends.
Inputs may be any that keep to these rules, and one draw needn't show every extreme that they name: `task_count`: the counts of two devices with the same sector index whose term indices differ by half the term axis add up to 8.
All inputs are finite; a program needn't handle non-finite values.
Results may differ from the reference program's by a relative error of at most 0.0003.
Values sent between devices are 32-bit elements; how exact they have to be, the bound alone decides.
No kernel may reach another device: no remote copies, remote signals or barrier semaphores. Data moves between devices by JAX's collectives and lax.ppermute only.
A program may use at most 64 MiB of HBM per device.

```python
import math
import jax
import jax.numpy as jnp
from jax import lax

B = 512
SEC_DEV = 2
CAP = 8
STEPS = 3
SECTORS = 8
SLOTS = 256
N_TERM = 8
DEVICES = 32


def draw_sector_dims(key, part):
    values = jax.random.randint(jax.random.fold_in(key, 11), (SECTORS,), B // 4, B + 1, dtype=jnp.int32)
    index = jnp.arange(SECTORS, dtype=jnp.int32)
    return jnp.where(index == 0, B, values)


def draw_task_count(key, part):
    values = jax.random.randint(jax.random.fold_in(key, 23), (DEVICES,), 1, CAP, dtype=jnp.int32)
    index = jnp.arange(DEVICES, dtype=jnp.int32)
    values = jnp.where(index == 0, CAP - 1, values)
    half = N_TERM // 2
    lower = index % N_TERM < half
    partner = jnp.where(lower, index, index - half)
    paired = values[partner]
    return jnp.where(lower, paired, CAP - paired)


def with_ends(array, own_key, low, top_value):
    longest = array.shape.index(max(array.shape))
    spots = []
    for shift in (0, 1):
        where = [jax.random.randint(jax.random.fold_in(own_key, axis), (), 0, length) for axis, length in enumerate(array.shape)]
        where[longest] = (where[longest] + shift) % array.shape[longest]
        spots.append(tuple(where))
    return array.at[spots[0]].set(low).at[spots[1]].set(top_value)


def block_scale(rng, dims, shards, low, high):
    def one(dim, shards_of):
        steps = jax.random.uniform(jax.random.fold_in(jax.random.fold_in(rng, 6), dim), (shards_of,), jnp.float32, low / len(shards), high / len(shards))
        return jnp.repeat(jnp.exp(steps), dims[dim] // shards_of).reshape((-1,) + (1,) * (len(dims) - dim - 1))

    factor_of = one(*shards[0])
    for cut in shards[1:]:
        factor_of = factor_of * one(*cut)
    return factor_of


def scatter_about(own_key, shape, deviation, reach, split=(), kind=jnp.bfloat16):
    values = deviation * jax.random.normal(own_key, shape, jnp.float32)
    if split:
        values = values * block_scale(own_key, shape, split, -0.22, 0.18)
    return jnp.clip(values, -reach, reach).astype(kind)


def setup_inputs(seed: int = 0) -> dict:
    streams_of = jax.random.split(jax.random.key(seed), 9)
    return {
        "trial": scatter_about(streams_of[0], (SECTORS, B, B), 1.0, 6.0, ((0, 4), (1, 8)), jnp.float32),
        "precond": jnp.clip(jnp.exp(math.log(16.0) - 2.0794415 * jax.random.uniform(streams_of[1], (SECTORS, B, B), jnp.float32) ** block_scale(streams_of[1], (SECTORS, B, B), ((0, 4), (1, 8)), -0.2, 0.2)), 2.0, 16.0),
        "sector_dims": draw_sector_dims(jax.random.fold_in(streams_of[8], 71), 0),
        "left_ops": scatter_about(streams_of[3], (SLOTS, B, B), B ** -0.5, 0.25, ((0, 32),), jnp.float32),
        "right_ops": scatter_about(streams_of[4], (SLOTS, B, B), B ** -0.5, 0.25, ((0, 32),), jnp.float32),
        "task_source": with_ends(jax.random.randint(streams_of[5], (SLOTS,), 0, SEC_DEV), jax.random.fold_in(streams_of[5], 1), 0, SEC_DEV - 1).astype(jnp.int32),
        "task_target": with_ends(jax.random.randint(streams_of[6], (SLOTS,), 0, SEC_DEV), jax.random.fold_in(streams_of[6], 1), 0, SEC_DEV - 1).astype(jnp.int32),
        "task_count": draw_task_count(jax.random.fold_in(streams_of[8], 71), 0),
    }


def reference(trial, precond, sector_dims, left_ops, right_ops, task_source, task_target, task_count):
    index = jnp.arange(B, dtype=jnp.int32)
    inside = index[None, :] < sector_dims[:, None]
    mask = (inside[:, :, None] & inside[:, None, :]).astype(trial.dtype)
    cells = SECTORS * B * B
    highest = lax.Precision.HIGHEST

    def rescale(u):
        return u * jnp.sqrt(cells / jnp.sum(u * u))

    def sigma_of(vector):

        def one(acc, items):
            left, right, source, target, slot = items
            device = slot // CAP
            group = device // N_TERM
            live = slot % CAP < task_count[device]
            src = (group * SEC_DEV + source).astype(jnp.int32)
            tgt = (group * SEC_DEV + target).astype(jnp.int32)

            def work(total):
                block = lax.dynamic_index_in_dim(vector, src, 0, keepdims=False)
                inner = jnp.dot(block, right, precision=highest)
                product = jnp.dot(left, inner, precision=highest)
                old = lax.dynamic_index_in_dim(total, tgt, 0, keepdims=True)
                return lax.dynamic_update_index_in_dim(total, old + product[None], tgt, 0)
            return (lax.cond(live, work, lambda total: total, acc), None)
        slots = jnp.arange(SLOTS, dtype=jnp.int32)
        acc, _ = lax.scan(one, jnp.zeros_like(vector), (left_ops, right_ops, task_source, task_target, slots))
        return acc * mask
    vector = rescale(mask * trial)
    values = []
    for step in range(STEPS):
        sig = sigma_of(vector)
        theta = jnp.sum(vector * sig) / jnp.sum(vector * vector)
        values.append(theta)
        vector = rescale(vector - (sig - theta * vector) / precond)
    return (vector, jnp.stack(values))
```

```python
import functools

import jax
import jax.numpy as jnp
from jax import lax
from jax.experimental import pallas as pl
from jax.experimental.pallas import tpu as pltpu
from jax.sharding import PartitionSpec as P

STEPS = 3
VMEM_LIMIT = 48 * 1024 * 1024
F32 = jnp.float32
BF16 = jnp.bfloat16


def live_slot(slots):
    return lambda k, info: (jnp.minimum(k, info[2 * slots + 2] - 1), 0, 0)


def split(value):
    high = value.astype(BF16)
    return high, (value - high.astype(F32)).astype(BF16)


def dot3(a_high, a_low, b_high, b_low):
    def dot(a, b):
        return jnp.dot(a, b, preferred_element_type=F32)

    return dot(a_high, b_high) + (dot(a_high, b_low) + dot(a_low, b_high))


def split_kernel(slots, info, left, right, left_high, left_low, right_high, right_low):
    @pl.when(pl.program_id(0) < info[2 * slots + 2])
    def _():
        left_high[...], left_low[...] = split(left[...])
        right_high[...], right_low[...] = split(right[...])


def split_operators(info, lefts, rights):
    slots, width, _ = lefts.shape
    live = live_slot(slots)
    spec = pl.BlockSpec((1, width, width), live)
    return pl.pallas_call(
        functools.partial(split_kernel, slots),
        grid_spec=pltpu.PrefetchScalarGridSpec(
            num_scalar_prefetch=1, grid=(slots - 1,), in_specs=[spec] * 2, out_specs=[spec] * 4
        ),
        out_shape=[jax.ShapeDtypeStruct(lefts.shape, BF16)] * 4,
        compiler_params=pltpu.CompilerParams(vmem_limit_bytes=VMEM_LIMIT),
        cost_estimate=pl.CostEstimate(
            flops=slots * width * width * 4, bytes_accessed=slots * width * width * 16, transcendentals=0
        ),
        name="split_operators",
    )(info, lefts, rights)


def split_blocks(blocks, high, low):
    share = blocks[0].shape[1]
    for place, block in enumerate(blocks):
        rows = pl.ds(place * share, share)
        high[:, rows, :], low[:, rows, :] = split(block[...])


def inner_kernel(slots, ring, info, *refs):
    blocks = refs[:ring]
    right_high, right_low, out_high, out_low, high, low = refs[ring:]
    k = pl.program_id(0)

    @pl.when(k == 0)
    def _():
        split_blocks(blocks, high, low)

    @pl.when(k < info[2 * slots + 2])
    def _():
        source = info[k]
        out_high[0], out_low[0] = split(
            dot3(high[source], low[source], right_high[0], right_low[0])
        )


def inner_rows(info, blocks, right_high, right_low):
    ring = len(blocks)
    slots, width, _ = right_high.shape
    live = live_slot(slots)
    sectors, share, _ = blocks[0].shape
    rows = ring * share
    whole = pl.BlockSpec((sectors, share, width), lambda k, info: (0, 0, 0))
    operator = pl.BlockSpec((1, width, width), live)
    result = pl.BlockSpec((1, rows, width), live)
    return pl.pallas_call(
        functools.partial(inner_kernel, slots, ring),
        grid_spec=pltpu.PrefetchScalarGridSpec(
            num_scalar_prefetch=1,
            grid=(slots - 1,),
            in_specs=[whole] * ring + [operator] * 2,
            out_specs=[result] * 2,
            scratch_shapes=[pltpu.VMEM((sectors, rows, width), BF16)] * 2,
        ),
        out_shape=[jax.ShapeDtypeStruct((slots, rows, width), BF16)] * 2,
        compiler_params=pltpu.CompilerParams(vmem_limit_bytes=VMEM_LIMIT),
        cost_estimate=pl.CostEstimate(
            flops=slots * rows * width * width * 6,
            bytes_accessed=slots * width * width * 4,
            transcendentals=0,
        ),
        name="inner_rows",
    )(info, *blocks, right_high, right_low)


def place_of(info, slots, ring, share, offset, side):
    around = lax.rem(info[2 * slots] + offset, ring)
    return pl.multiple_of((around * 2 + side) * share, share)


def outer_rows(info, slots, ring, side, left_high, left_low, high, low, outs, k):
    share = outs[0].shape[1]
    picks = [pl.ds(place_of(info, slots, ring, share, r, side), share) for r in range(ring)]
    lefts_high = jnp.concatenate([left_high[0, pick, :] for pick in picks], axis=0)
    lefts_low = jnp.concatenate([left_low[0, pick, :] for pick in picks], axis=0)
    product = dot3(lefts_high, lefts_low, high, low)
    target = info[slots + k]
    for r in range(ring):
        outs[r][target] += product[r * share : (r + 1) * share]


def overlap_sum(blocks, outs):
    total = jnp.zeros((1, blocks[0].shape[2]), F32)
    for block, out in zip(blocks, outs):
        for sector in range(block.shape[0]):
            total = total + jnp.sum(block[sector] * out[sector], axis=0, keepdims=True)
    return jnp.broadcast_to(total, (8, total.shape[1]))


def middle_kernel(slots, ring, info, *refs):
    blocks, refs = refs[:ring], refs[ring:]
    part_high, part_low, right_high, right_low, left_high, left_low = refs[:6]
    full_high, full_low, dots = refs[6:9]
    outs = refs[9 : 9 + ring]
    high, low = refs[9 + ring :]
    k = pl.program_id(0)
    share = blocks[0].shape[1]
    side = info[2 * slots + 1]

    @pl.when(k == 0)
    def _():
        split_blocks(blocks, high, low)
        for out in outs:
            out[...] = jnp.zeros_like(out)

    @pl.when(k < info[2 * slots + 2])
    def _():
        source = info[k]
        inner_high, inner_low = split(
            dot3(high[source], low[source], right_high[0], right_low[0])
        )
        for r in range(ring):
            own = pl.ds(place_of(info, slots, ring, share, r, side), share)
            other = pl.ds(place_of(info, slots, ring, share, r, 1 - side), share)
            rows = slice(r * share, (r + 1) * share)
            full_high[0, own, :] = part_high[0, rows, :]
            full_low[0, own, :] = part_low[0, rows, :]
            full_high[0, other, :] = inner_high[rows]
            full_low[0, other, :] = inner_low[rows]
        outer_rows(
            info, slots, ring, 1 - side, left_high, left_low, full_high[0], full_low[0], outs, k
        )

    @pl.when(k == pl.num_programs(0) - 1)
    def _():
        dots[...] = overlap_sum(blocks, outs)


def middle(info, blocks, part, right, left):
    ring = len(blocks)
    slots, width, _ = right[0].shape
    live = live_slot(slots)
    sectors, share, _ = blocks[0].shape
    rows = ring * share
    whole = pl.BlockSpec((sectors, share, width), lambda k, info: (0, 0, 0))
    operator = pl.BlockSpec((1, width, width), live)
    partial = pl.BlockSpec((1, rows, width), live)
    fixed = pl.BlockSpec((8, width), lambda k, info: (0, 0))
    results = pl.pallas_call(
        functools.partial(middle_kernel, slots, ring),
        grid_spec=pltpu.PrefetchScalarGridSpec(
            num_scalar_prefetch=1,
            grid=(slots - 1,),
            in_specs=[whole] * ring + [partial] * 2 + [operator] * 4,
            out_specs=[operator] * 2 + [fixed] + [whole] * ring,
            scratch_shapes=[pltpu.VMEM((sectors, rows, width), BF16)] * 2,
        ),
        out_shape=[jax.ShapeDtypeStruct((slots, width, width), BF16)] * 2
        + [jax.ShapeDtypeStruct((8, width), F32)]
        + [jax.ShapeDtypeStruct(blocks[0].shape, F32)] * ring,
        compiler_params=pltpu.CompilerParams(vmem_limit_bytes=VMEM_LIMIT),
        cost_estimate=pl.CostEstimate(
            flops=slots * rows * width * width * 12,
            bytes_accessed=slots * width * width * 16,
            transcendentals=0,
        ),
        name="middle",
    )(info, *blocks, *part, *right, *left)
    return results[:2], results[2], results[3:]


def outer_kernel(slots, ring, info, *refs):
    blocks, refs = refs[:ring], refs[ring:]
    full_high, full_low, left_high, left_low, dots = refs[:5]
    outs = refs[5:]
    k = pl.program_id(0)

    @pl.when(k == 0)
    def _():
        for out in outs:
            out[...] = jnp.zeros_like(out)

    @pl.when(k < info[2 * slots + 2])
    def _():
        outer_rows(
            info, slots, ring, info[2 * slots + 1], left_high, left_low, full_high[0], full_low[0], outs, k
        )

    @pl.when(k == pl.num_programs(0) - 1)
    def _():
        dots[...] = overlap_sum(blocks, outs)


def outer_own(info, blocks, full, left):
    ring = len(blocks)
    slots, width, _ = left[0].shape
    live = live_slot(slots)
    sectors, share, _ = blocks[0].shape
    whole = pl.BlockSpec((sectors, share, width), lambda k, info: (0, 0, 0))
    operator = pl.BlockSpec((1, width, width), live)
    fixed = pl.BlockSpec((8, width), lambda k, info: (0, 0))
    results = pl.pallas_call(
        functools.partial(outer_kernel, slots, ring),
        grid_spec=pltpu.PrefetchScalarGridSpec(
            num_scalar_prefetch=1,
            grid=(slots - 1,),
            in_specs=[whole] * ring + [operator] * 4,
            out_specs=[fixed] + [whole] * ring,
        ),
        out_shape=[jax.ShapeDtypeStruct((8, width), F32)]
        + [jax.ShapeDtypeStruct(blocks[0].shape, F32)] * ring,
        compiler_params=pltpu.CompilerParams(vmem_limit_bytes=VMEM_LIMIT),
        cost_estimate=pl.CostEstimate(
            flops=slots * ring * share * width * width * 6,
            bytes_accessed=slots * width * width * 8,
            transcendentals=0,
        ),
        name="outer_own",
    )(info, *blocks, *full, *left)
    return results[0], results[1:]


def across(value, terms):
    return lax.ppermute(value, "term", [(i, i ^ 1) for i in range(terms)])


def around(value, terms, shift):
    return lax.ppermute(value, "term", [(i, (i + 2 * shift) % terms) for i in range(terms)])


def gather_own(block, terms):
    ring = terms // 2
    blocks = {0: block}
    ups = ring // 2
    downs = ring - 1 - ups
    for hop in range(1, ups + 1):
        blocks[(ring - hop) % ring] = around(blocks[(ring - hop + 1) % ring], terms, 1)
        if hop <= downs:
            blocks[hop] = around(blocks[hop - 1], terms, -1)
    return [blocks[r] for r in range(ring)]


def total_sum(values, sectors, terms):
    for axis, size in (("sector", sectors), ("term", terms)):
        if size & (size - 1):
            values = lax.psum(values, axis)
            continue
        step = 1
        while step < size:
            values = values + lax.ppermute(values, axis, [(i, i ^ step) for i in range(size)])
            step *= 2
    return values


def scatter_sum(own, other, terms):
    ring = terms // 2
    ups = ring // 2
    downs = ring - 1 - ups
    order = []
    for hop in range(ups, 0, -1):
        order.append(hop)
        if hop <= downs:
            order.append((ring - hop) % ring)
    order.append(0)
    received = {r: across(other[r], terms) for r in order}
    pair = {}
    for r in order:
        pair[r] = own[r] + received[r]
    up = down = None
    for hop in range(ups, 0, -1):
        value = pair[hop] if up is None else pair[hop] + up
        up = around(value, terms, 1)
        if hop <= downs:
            value = pair[(ring - hop) % ring] if down is None else pair[(ring - hop) % ring] + down
            down = around(value, terms, -1)
    total = pair[0]
    if up is not None:
        total = total + up
    if down is not None:
        total = total + down
    return total


def per_device(
    trial, precond, sector_dims, left_ops, right_ops, task_source, task_target, task_count
):
    sec_dev, share, width = trial.shape
    sectors, terms = lax.axis_size("sector"), lax.axis_size("term")
    ring = terms // 2
    cells = float(sec_dev * sectors * width * width)
    term = lax.axis_index("term").astype(jnp.int32)
    rows = term * share + jnp.arange(share, dtype=jnp.int32)
    cols = jnp.arange(width, dtype=jnp.int32)
    limits = sector_dims[:, None]
    mask = ((rows[None, :] < limits)[:, :, None] & (cols[None, :] < limits)[:, None, :]).astype(F32)
    info = jnp.concatenate([task_source, task_target, jnp.stack([term // 2, term % 2, task_count[0]])])
    values = []
    vector = mask * trial
    parts = split_operators(info, left_ops, right_ops)
    left, right = parts[:2], parts[2:]
    for step in range(STEPS):
        mine = gather_own(vector, terms)
        theirs = [across(block, terms) for block in mine]
        part = inner_rows(info, mine, *right)
        full, dots_other, outs_other = middle(info, theirs, part, right, left)
        dots_own, outs_own = outer_own(info, mine, full, left)
        dots = jnp.sum(dots_own[0] + dots_other[0])
        sums = total_sum(jnp.stack([dots, jnp.sum(vector * vector)]), sectors, terms)
        theta = sums[0] / sums[1]
        values.append(theta)
        sig = scatter_sum(outs_own, outs_other, terms) * mask
        vector = vector - (sig - theta * vector) / precond
    total = total_sum(jnp.sum(vector * vector)[None], sectors, terms)
    return (vector * jnp.sqrt(cells / total[0]), jnp.stack(values))


def solution(mesh):
    return jax.shard_map(
        per_device,
        mesh=mesh,
        in_specs=(
            P("sector", "term", None),
            P("sector", "term", None),
            P("sector"),
            P(("sector", "term"), None, None),
            P(("sector", "term"), None, None),
            P(("sector", "term")),
            P(("sector", "term")),
            P(("sector", "term")),
        ),
        out_specs=(P("sector", "term", None), P()),
        check_vma=False,
    )
```

```python
import functools

import jax
import jax.numpy as jnp
from jax import lax
from jax.experimental import pallas as pl
from jax.experimental.pallas import tpu as pltpu
from jax.sharding import PartitionSpec as P

STEPS = 3
VMEM_LIMIT = 14 * 1024 * 1024
F32 = jnp.float32
BF16 = jnp.bfloat16


def split(value):
    high = value.astype(BF16)
    return high, (value - high.astype(F32)).astype(BF16)


def dot3(a_high, a_low, b_high, b_low):
    def dot(a, b):
        return jnp.dot(a, b, preferred_element_type=F32)

    return dot(a_high, b_high) + (dot(a_high, b_low) + dot(a_low, b_high))


def call(kernel, name, info, arrays, results, flops, scratch=()):
    held = pl.BlockSpec(memory_space=pltpu.VMEM)
    return pl.pallas_call(
        kernel,
        in_specs=[pl.BlockSpec(memory_space=pltpu.SMEM)] + [held] * len(arrays),
        out_specs=[held] * len(results),
        out_shape=[pltpu.VMEM(shape, dtype) for shape, dtype in results],
        scratch_shapes=list(scratch),
        compiler_params=pltpu.CompilerParams(vmem_limit_bytes=VMEM_LIMIT),
        cost_estimate=pl.CostEstimate(flops=flops, bytes_accessed=0, transcendentals=0),
        name=name,
    )(info, *arrays)


class Place:
    def __init__(self, slots):
        self.target, self.ring, self.side = slots, 2 * slots, 2 * slots + 1
        self.count, self.limits = 2 * slots + 2, 2 * slots + 3


def split_kernel(at, info, operator, high, low):
    k = pl.program_id(0)

    @pl.when(k < info[at.count])
    def _():
        high[k], low[k] = split(operator[0])


def split_operators(info, operators, name):
    slots, width, _ = operators.shape
    at = Place(slots)
    return pl.pallas_call(
        functools.partial(split_kernel, at),
        grid_spec=pltpu.PrefetchScalarGridSpec(
            num_scalar_prefetch=1,
            grid=(slots - 1,),
            in_specs=[
                pl.BlockSpec(
                    (1, width, width), lambda k, info: (jnp.minimum(k, info[at.count] - 1), 0, 0)
                )
            ],
            out_specs=[pl.BlockSpec(memory_space=pltpu.VMEM)] * 2,
        ),
        out_shape=[pltpu.VMEM((slots - 1, width, width), BF16)] * 2,
        compiler_params=pltpu.CompilerParams(vmem_limit_bytes=VMEM_LIMIT),
        cost_estimate=pl.CostEstimate(
            flops=0, bytes_accessed=slots * width * width * 4, transcendentals=0
        ),
        name=name,
    )(info, operators)


def split_blocks(blocks, high, low):
    share = blocks[0].shape[1]
    for place, block in enumerate(blocks):
        rows = pl.ds(place * share, share)
        high[:, rows, :], low[:, rows, :] = split(block[...])


def lanes(value):
    total = jnp.sum(value, axis=tuple(range(value.ndim - 1)))[None]
    width = total.shape[1]
    return sum(total[:, c : c + 128] for c in range(0, width, 128))


def inner_kernel(at, ring, info, *refs):
    blocks = refs[:ring]
    right_high, right_low, out_high, out_low, high, low = refs[ring:]
    split_blocks(blocks, high, low)

    def one(k, carry):
        source = info[k]
        out_high[k], out_low[k] = split(
            dot3(high[source], low[source], right_high[k], right_low[k])
        )
        return carry

    lax.fori_loop(0, info[at.count], one, 0)


def inner_rows(at, info, blocks, right):
    ring = len(blocks)
    live, width, _ = right[0].shape
    sectors, share, _ = blocks[0].shape
    rows = ring * share
    return call(
        functools.partial(inner_kernel, at, ring),
        "inner_rows",
        info,
        [*blocks, *right],
        [((live, rows, width), BF16)] * 2,
        live * rows * width * width * 6,
        [pltpu.VMEM((sectors, rows, width), BF16)] * 2,
    )


def first_row(at, info, ring, share, offset, side):
    around = lax.rem(info[at.ring] + offset, ring)
    return pl.multiple_of((around * 2 + side) * share, share)


def outer_rows(at, info, k, ring, side, left, full, outs):
    share = outs[0].shape[1]
    picks = [pl.ds(first_row(at, info, ring, share, r, side), share) for r in range(ring)]
    high, low = (
        jnp.concatenate([part[k, pick, :] for pick in picks], axis=0) for part in left
    )
    product = dot3(high, low, full[0][k], full[1][k])
    target = info[at.target + k]
    for r in range(ring):
        outs[r][target] += product[r * share : (r + 1) * share]


def overlap(blocks, outs):
    return sum(lanes(block[...] * out[...]) for block, out in zip(blocks, outs))


def middle_kernel(at, ring, info, *refs):
    blocks, refs = refs[:ring], refs[ring:]
    part_high, part_low, right_high, right_low, left_high, left_low = refs[:6]
    full_high, full_low, dots = refs[6:9]
    outs = refs[9 : 9 + ring]
    high, low = refs[9 + ring :]
    share = blocks[0].shape[1]
    side = info[at.side]
    split_blocks(blocks, high, low)
    for out in outs:
        out[...] = jnp.zeros_like(out)

    def one(k, carry):
        source = info[k]
        inner_high, inner_low = split(
            dot3(high[source], low[source], right_high[k], right_low[k])
        )
        for r in range(ring):
            own = pl.ds(first_row(at, info, ring, share, r, side), share)
            other = pl.ds(first_row(at, info, ring, share, r, 1 - side), share)
            rows = slice(r * share, (r + 1) * share)
            full_high[k, own, :] = part_high[k, rows, :]
            full_low[k, own, :] = part_low[k, rows, :]
            full_high[k, other, :] = inner_high[rows]
            full_low[k, other, :] = inner_low[rows]
        outer_rows(
            at, info, k, ring, 1 - side, (left_high, left_low), (full_high, full_low), outs
        )
        return carry

    lax.fori_loop(0, info[at.count], one, 0)
    dots[...] = overlap(blocks, outs)


def middle(at, info, blocks, part, right, left):
    ring = len(blocks)
    live, width, _ = right[0].shape
    sectors, share, _ = blocks[0].shape
    rows = ring * share
    results = call(
        functools.partial(middle_kernel, at, ring),
        "middle",
        info,
        [*blocks, *part, *right, *left],
        [((live, width, width), BF16)] * 2 + [((1, 128), F32)] + [(blocks[0].shape, F32)] * ring,
        live * rows * width * width * 12,
        [pltpu.VMEM((sectors, rows, width), BF16)] * 2,
    )
    return results[:2], results[2], results[3:]


def outer_kernel(at, ring, info, *refs):
    blocks, refs = refs[:ring], refs[ring:]
    full_high, full_low, left_high, left_low, dots_other, squares, sums = refs[:7]
    outs = refs[7:]
    for out in outs:
        out[...] = jnp.zeros_like(out)

    def one(k, carry):
        outer_rows(
            at, info, k, ring, info[at.side], (left_high, left_low), (full_high, full_low), outs
        )
        return carry

    lax.fori_loop(0, info[at.count], one, 0)
    row = lax.broadcasted_iota(jnp.int32, sums.shape, 0)
    dots = overlap(blocks, outs) + dots_other[...]
    sums[...] = jnp.where(row == 0, dots, jnp.where(row == 1, squares[...], 0.0))


def outer_own(at, info, blocks, full, left, dots_other, squares):
    ring = len(blocks)
    live, width, _ = left[0].shape
    share = blocks[0].shape[1]
    results = call(
        functools.partial(outer_kernel, at, ring),
        "outer_own",
        info,
        [*blocks, *full, *left, dots_other, squares],
        [((8, 128), F32)] + [(blocks[0].shape, F32)] * ring,
        live * ring * share * width * width * 6,
    )
    return results[0], results[1:]


def inside(at, info, shape, ring):
    share = shape[1]
    start = (info[at.ring] * 2 + info[at.side]) * share
    rows = start + lax.broadcasted_iota(jnp.int32, shape[1:], 0)
    cols = lax.broadcasted_iota(jnp.int32, shape[1:], 1)
    return [
        ((rows < info[at.limits + s]) & (cols < info[at.limits + s])).astype(F32)
        for s in range(shape[0])
    ]


def begin_kernel(at, ring, info, trial, vector, squares):
    total = jnp.zeros(squares.shape, F32)
    for s, mask in enumerate(inside(at, info, trial.shape, ring)):
        value = mask * trial[s]
        vector[s] = value
        total = total + lanes(value * value)
    squares[...] = total


def begin(at, info, trial, ring):
    return call(
        functools.partial(begin_kernel, at, ring),
        "begin",
        info,
        [trial],
        [(trial.shape, F32), ((1, 128), F32)],
        trial.size * 4,
    )


def update_kernel(at, ring, info, *refs):
    vector, precond, sums = refs[:3]
    terms, (result, squares, ritz) = refs[3:-3], refs[-3:]
    both = jnp.sum(sums[...], axis=1, keepdims=True)
    theta = both[0:1] / both[1:2]
    ritz[...] = jnp.broadcast_to(theta, ritz.shape)
    total = jnp.zeros(squares.shape, F32)
    for s, mask in enumerate(inside(at, info, vector.shape, ring)):
        sig = mask * sum(term[s] for term in terms)
        value = vector[s] - (sig - theta * vector[s]) / precond[s]
        result[s] = value
        total = total + lanes(value * value)
    squares[...] = total


def update(at, info, vector, precond, sums, terms, ring):
    return call(
        functools.partial(update_kernel, at, ring),
        "update",
        info,
        [vector, precond, sums, *terms],
        [(vector.shape, F32), ((1, 128), F32), ((1, 128), F32)],
        vector.size * 8,
    )


def across(value, terms):
    return lax.ppermute(value, "term", [(i, i ^ 1) for i in range(terms)])


def around(value, terms, shift):
    return lax.ppermute(value, "term", [(i, (i + 2 * shift) % terms) for i in range(terms)])


def gather_own(block, terms):
    ring = terms // 2
    blocks = {0: block}
    ups = ring // 2
    downs = ring - 1 - ups
    for hop in range(1, ups + 1):
        blocks[(ring - hop) % ring] = around(blocks[(ring - hop + 1) % ring], terms, 1)
        if hop <= downs:
            blocks[hop] = around(blocks[hop - 1], terms, -1)
    return [blocks[r] for r in range(ring)]


def total_sum(values, sectors, terms):
    for axis, size in (("sector", sectors), ("term", terms)):
        if size & (size - 1):
            values = lax.psum(values, axis)
            continue
        step = 1
        while step < size:
            values = values + lax.ppermute(values, axis, [(i, i ^ step) for i in range(size)])
            step *= 2
    return values


def scatter_sum(own, other, terms):
    ring = terms // 2
    ups = ring // 2
    downs = ring - 1 - ups
    order = []
    for hop in range(ups, 0, -1):
        order.append(hop)
        if hop <= downs:
            order.append((ring - hop) % ring)
    order.append(0)
    received = {r: across(other[r], terms) for r in order}
    up = down = None
    for hop in range(ups, 0, -1):
        value = own[hop] + received[hop]
        up = around(value if up is None else value + up, terms, 1)
        if hop <= downs:
            back = (ring - hop) % ring
            value = own[back] + received[back]
            down = around(value if down is None else value + down, terms, -1)
    return [term for term in (own[0], received[0], up, down) if term is not None]


def per_device(
    trial, precond, sector_dims, left_ops, right_ops, task_source, task_target, task_count
):
    sec_dev, share, width = trial.shape
    slots = left_ops.shape[0]
    sectors, terms = lax.axis_size("sector"), lax.axis_size("term")
    ring = terms // 2
    cells = float(sec_dev * sectors * width * width)
    term = lax.axis_index("term").astype(jnp.int32)
    at = Place(slots)
    info = jnp.concatenate(
        [task_source, task_target, jnp.stack([term // 2, term % 2]), task_count, sector_dims]
    )
    values = []
    vector, squares = begin(at, info, trial, ring)
    right = split_operators(info, right_ops, "split_right")
    left = split_operators(info, left_ops, "split_left")
    for step in range(STEPS):
        mine = gather_own(vector, terms)
        theirs = [across(block, terms) for block in mine]
        part = inner_rows(at, info, mine, right)
        full, dots_other, outs_other = middle(at, info, theirs, part, right, left)
        sums, outs_own = outer_own(at, info, mine, full, left, dots_other, squares)
        sums = total_sum(sums, sectors, terms)
        summed = scatter_sum(outs_own, outs_other, terms)
        vector, squares, ritz = update(at, info, vector, precond, sums, summed, ring)
        values.append(ritz[0, :1])
    total = jnp.sum(total_sum(squares, sectors, terms))
    return (vector * jnp.sqrt(cells / total), jnp.concatenate(values))


def solution(mesh):
    return jax.shard_map(
        per_device,
        mesh=mesh,
        in_specs=(
            P("sector", "term", None),
            P("sector", "term", None),
            P("sector"),
            P(("sector", "term"), None, None),
            P(("sector", "term"), None, None),
            P(("sector", "term")),
            P(("sector", "term")),
            P(("sector", "term")),
        ),
        out_specs=(P("sector", "term", None), P()),
        check_vma=False,
    )
```

```python
import functools

import jax
import jax.numpy as jnp
from jax import lax
from jax.experimental import pallas as pl
from jax.experimental.pallas import tpu as pltpu
from jax.sharding import PartitionSpec as P

STEPS = 3
VMEM_LIMIT = 14 * 1024 * 1024
F32 = jnp.float32
BF16 = jnp.bfloat16


def split(value):
    high = value.astype(BF16)
    return high, (value - high.astype(F32)).astype(BF16)


def dot3(a_high, a_low, b_high, b_low):
    def dot(a, b):
        return jnp.dot(a, b, preferred_element_type=F32)

    return dot(a_high, b_high) + (dot(a_high, b_low) + dot(a_low, b_high))


def call(kernel, name, info, arrays, results, flops, scratch=()):
    held = pl.BlockSpec(memory_space=pltpu.VMEM)
    return pl.pallas_call(
        kernel,
        in_specs=[pl.BlockSpec(memory_space=pltpu.SMEM)] + [held] * len(arrays),
        out_specs=[held] * len(results),
        out_shape=[pltpu.VMEM(shape, dtype) for shape, dtype in results],
        scratch_shapes=list(scratch),
        compiler_params=pltpu.CompilerParams(vmem_limit_bytes=VMEM_LIMIT),
        cost_estimate=pl.CostEstimate(flops=flops, bytes_accessed=0, transcendentals=0),
        name=name,
    )(info, *arrays)


class Place:
    def __init__(self, slots):
        self.target, self.ring, self.side = slots, 2 * slots, 2 * slots + 1
        self.count, self.limits = 2 * slots + 2, 2 * slots + 3


def split_kernel(at, info, operator, *refs):
    high, low = refs[-2:]
    k = pl.program_id(0)

    @pl.when(k < info[at.count])
    def _():
        high[k], low[k] = split(operator[0])


def split_operators(info, operators, earlier, name):
    slots, width, _ = operators.shape
    at = Place(slots)
    return pl.pallas_call(
        functools.partial(split_kernel, at),
        grid_spec=pltpu.PrefetchScalarGridSpec(
            num_scalar_prefetch=1,
            grid=(slots - 1,),
            in_specs=[
                pl.BlockSpec(
                    (1, width, width), lambda k, info: (jnp.minimum(k, info[at.count] - 1), 0, 0)
                )
            ]
            + [pl.BlockSpec(memory_space=pltpu.VMEM)] * len(earlier),
            out_specs=[pl.BlockSpec(memory_space=pltpu.VMEM)] * 2,
        ),
        out_shape=[pltpu.VMEM((slots - 1, width, width), BF16)] * 2,
        compiler_params=pltpu.CompilerParams(vmem_limit_bytes=VMEM_LIMIT),
        cost_estimate=pl.CostEstimate(
            flops=0, bytes_accessed=slots * width * width * 4, transcendentals=0
        ),
        name=name,
    )(info, operators, *earlier)


def split_blocks(blocks, high, low):
    share = blocks[0].shape[1]
    for place, block in enumerate(blocks):
        rows = pl.ds(place * share, share)
        high[:, rows, :], low[:, rows, :] = split(block[...])


def lanes(value):
    total = jnp.sum(value, axis=tuple(range(value.ndim - 1)))[None]
    width = total.shape[1]
    return sum(total[:, c : c + 128] for c in range(0, width, 128))


def inner_kernel(at, ring, info, *refs):
    blocks = refs[:ring]
    right_high, right_low = refs[ring : ring + 2]
    out_high, out_low, high, low = refs[-4:]
    split_blocks(blocks, high, low)

    def one(k, carry):
        source = info[k]
        out_high[k], out_low[k] = split(
            dot3(high[source], low[source], right_high[k], right_low[k])
        )
        return carry

    lax.fori_loop(0, info[at.count], one, 0)


def inner_rows(at, info, blocks, right, earlier=()):
    ring = len(blocks)
    live, width, _ = right[0].shape
    sectors, share, _ = blocks[0].shape
    rows = ring * share
    return call(
        functools.partial(inner_kernel, at, ring),
        "inner_rows",
        info,
        [*blocks, *right, *earlier],
        [((live, rows, width), BF16)] * 2,
        live * rows * width * width * 6,
        [pltpu.VMEM((sectors, rows, width), BF16)] * 2,
    )


def first_row(at, info, ring, share, offset, side):
    around = lax.rem(info[at.ring] + offset, ring)
    return pl.multiple_of((around * 2 + side) * share, share)


def outer_rows(at, info, k, ring, places, left, full, outs):
    share = outs[0].shape[1]
    picks = [pl.ds(first_row(at, info, ring, share, *place), share) for place in places]
    high, low = (
        jnp.concatenate([part[k, pick, :] for pick in picks], axis=0) for part in left
    )
    product = dot3(high, low, full[0][k], full[1][k])
    target = info[at.target + k]
    for i, out in enumerate(outs):
        out[target] += product[i * share : (i + 1) * share]


def middle_kernel(at, ring, last, early, order, head, info, *refs):
    block, own_high, own_low, more_high, more_low = refs[:5]
    right_high, right_low, left_high, left_low = refs[5:9]
    full_high, full_low = refs[9:11]
    outs, (high, low) = refs[11:-2], refs[-2:]
    share = block.shape[1]
    side = info[at.side]
    split_blocks([block], high, low)
    for out in outs:
        out[...] = jnp.zeros_like(out)
    places = [(r, 1 - side) for r in order[: head[0]]] + [(r, side) for r in order[: head[1]]]

    def one(k, carry):
        source = info[k]
        inner = split(dot3(high[source], low[source], right_high[k], right_low[k]))
        for out, own, more, value in zip(
            (full_high, full_low), (own_high, own_low), (more_high, more_low), inner
        ):
            for r in range(ring):
                rows = pl.ds(first_row(at, info, ring, share, r, side), share)
                out[k, rows, :] = own[k, r * share : (r + 1) * share, :]
            for i, r in enumerate(early):
                rows = pl.ds(first_row(at, info, ring, share, r, 1 - side), share)
                out[k, rows, :] = more[k, i * share : (i + 1) * share, :]
            rows = pl.ds(first_row(at, info, ring, share, last, 1 - side), share)
            out[k, rows, :] = value
        outer_rows(
            at, info, k, ring, places, (left_high, left_low), (full_high, full_low), outs
        )
        return carry

    lax.fori_loop(0, info[at.count], one, 0)


def middle(at, info, ring, last, early, order, head, block, own, more, right, left):
    live, width, _ = right[0].shape
    sectors, share, _ = block.shape
    count = sum(head)
    results = call(
        functools.partial(middle_kernel, at, ring, last, early, order, head),
        "middle",
        info,
        [block, *own, *more, *right, *left],
        [((live, width, width), BF16)] * 2 + [(block.shape, F32)] * count,
        live * share * (1 + count) * width * width * 6,
        [pltpu.VMEM((sectors, share, width), BF16)] * 2,
    )
    return results[:2], results[2 : 2 + head[0]], results[2 + head[0] :]


def tail_kernel(at, ring, order, head, info, *refs):
    mine, theirs, refs = refs[:ring], refs[ring : 2 * ring], refs[2 * ring :]
    heads, refs = refs[: sum(head)], refs[sum(head) :]
    full_high, full_low, left_high, left_low, squares, sums = refs[:6]
    outs = refs[6:]
    side = info[at.side]
    for out in outs:
        out[...] = jnp.zeros_like(out)
    others, owns = order[head[0] :], order[head[1] :]
    places = [(r, 1 - side) for r in others] + [(r, side) for r in owns]

    def one(k, carry):
        outer_rows(
            at, info, k, ring, places, (left_high, left_low), (full_high, full_low), outs
        )
        return carry

    lax.fori_loop(0, info[at.count], one, 0)
    pairs = [(theirs[r], heads[i]) for i, r in enumerate(order[: head[0]])]
    pairs += [(mine[r], heads[head[0] + i]) for i, r in enumerate(order[: head[1]])]
    pairs += [(theirs[r], outs[i]) for i, r in enumerate(others)]
    pairs += [(mine[r], outs[len(others) + i]) for i, r in enumerate(owns)]
    dots = sum(lanes(block[...] * out[...]) for block, out in pairs)
    row = lax.broadcasted_iota(jnp.int32, sums.shape, 0)
    sums[...] = jnp.where(row == 0, dots, jnp.where(row == 1, squares[...], 0.0))


def tail(at, info, ring, order, head, mine, theirs, heads, full, left, squares):
    live, width, _ = left[0].shape
    share = mine[0].shape[1]
    count = 2 * ring - sum(head)
    results = call(
        functools.partial(tail_kernel, at, ring, order, head),
        "tail",
        info,
        [*mine, *theirs, *heads, *full, *left, squares],
        [((8, 128), F32)] + [(mine[0].shape, F32)] * count,
        0,
    )
    others = ring - head[0]
    return results[0], results[1 : 1 + others], results[1 + others :]


def inside(at, info, shape, ring):
    share = shape[1]
    start = (info[at.ring] * 2 + info[at.side]) * share
    rows = start + lax.broadcasted_iota(jnp.int32, shape[1:], 0)
    cols = lax.broadcasted_iota(jnp.int32, shape[1:], 1)
    return [
        ((rows < info[at.limits + s]) & (cols < info[at.limits + s])).astype(F32)
        for s in range(shape[0])
    ]


def begin_kernel(at, ring, info, trial, vector, squares):
    total = jnp.zeros(squares.shape, F32)
    for s, mask in enumerate(inside(at, info, trial.shape, ring)):
        value = mask * trial[s]
        vector[s] = value
        total = total + lanes(value * value)
    squares[...] = total


def begin(at, info, trial, ring):
    return call(
        functools.partial(begin_kernel, at, ring),
        "begin",
        info,
        [trial],
        [(trial.shape, F32), ((1, 128), F32)],
        trial.size * 4,
    )


def update_kernel(at, ring, info, *refs):
    vector, precond, sums = refs[:3]
    terms, (result, squares, ritz) = refs[3:-3], refs[-3:]
    both = jnp.sum(sums[...], axis=1, keepdims=True)
    theta = both[0:1] / both[1:2]
    ritz[...] = jnp.broadcast_to(theta, ritz.shape)
    total = jnp.zeros(squares.shape, F32)
    for s, mask in enumerate(inside(at, info, vector.shape, ring)):
        sig = mask * sum(term[s] for term in terms)
        value = vector[s] - (sig - theta * vector[s]) / precond[s]
        result[s] = value
        total = total + lanes(value * value)
    squares[...] = total


def update(at, info, vector, precond, sums, terms, ring):
    return call(
        functools.partial(update_kernel, at, ring),
        "update",
        info,
        [vector, precond, sums, *terms],
        [(vector.shape, F32), ((1, 128), F32), ((1, 128), F32)],
        vector.size * 8,
    )


def across(value, terms):
    return lax.ppermute(value, "term", [(i, i ^ 1) for i in range(terms)])


def around(value, terms, shift):
    return lax.ppermute(value, "term", [(i, (i + 2 * shift) % terms) for i in range(terms)])


def after(value, *tokens):
    return lax.optimization_barrier((value, *tokens))[0]


def gather_own(block, terms):
    ring = terms // 2
    blocks = {0: block}
    ups = ring // 2
    downs = ring - 1 - ups
    for hop in range(1, ups + 1):
        value = blocks[(ring - hop + 1) % ring]
        blocks[(ring - hop) % ring] = around(value, terms, 1)
        if hop <= downs:
            blocks[hop] = around(blocks[hop - 1], terms, -1)
    return [blocks[r] for r in range(ring)]


def stages(sectors, terms):
    return [
        (axis, size, 1 << bit)
        for axis, size in (("sector", sectors), ("term", terms))
        for bit in range(size.bit_length() - 1)
    ]


def stage_sum(values, stage):
    axis, size, step = stage
    return values + lax.ppermute(values, axis, [(i, i ^ step) for i in range(size)])


def send_order(ring):
    ups = ring // 2
    downs = ring - 1 - ups
    order = []
    for hop in range(ups, 0, -1):
        order.append(hop)
        if hop <= downs:
            order.append((ring - hop) % ring)
    return order + [0]


def scatter_sum(own, other, terms, sums, steps):
    ring = terms // 2
    ups = ring // 2
    downs = ring - 1 - ups
    received = {r: across(other[r], terms) for r in send_order(ring)}
    steps = list(steps)

    def advance(count):
        nonlocal sums
        for _ in range(min(count, len(steps))):
            sums = stage_sum(sums, steps.pop(0))
        return sums

    up = down = None
    for hop in range(ups, 0, -1):
        value = own[hop] + received[hop]
        up = around(after(value if up is None else value + up, advance(1)), terms, 1)
        if hop <= downs:
            back = (ring - hop) % ring
            value = own[back] + received[back]
            down = around(after(value if down is None else value + down, advance(1)), terms, -1)
    advance(len(steps))
    return [term for term in (own[0], received[0], up, down) if term is not None], sums


def per_device(
    trial, precond, sector_dims, left_ops, right_ops, task_source, task_target, task_count
):
    sec_dev, share, width = trial.shape
    slots = left_ops.shape[0]
    sectors, terms = lax.axis_size("sector"), lax.axis_size("term")
    ring = terms // 2
    cells = float(sec_dev * sectors * width * width)
    term = lax.axis_index("term").astype(jnp.int32)
    at = Place(slots)
    info = jnp.concatenate(
        [task_source, task_target, jnp.stack([term // 2, term % 2]), task_count, sector_dims]
    )
    values = []
    vector, squares = begin(at, info, trial, ring)
    steps = stages(sectors, terms)
    order = send_order(ring)
    last = ring - ring // 2
    early = [r for r in range(ring) if r != last]
    head = (ring // 2, ring // 4)
    for step in range(STEPS):
        mine = gather_own(vector, terms)
        if step == 0:
            arrived = [block for r, block in enumerate(mine) if r != last]
            right = split_operators(info, right_ops, arrived, "split_right")
            left = split_operators(info, left_ops, arrived, "split_left")
        theirs = [across(block, terms) for block in mine]
        own_rows = inner_rows(at, info, mine, right)
        more_rows = inner_rows(at, info, [theirs[r] for r in early], right, own_rows[:1])
        full, others, owns = middle(
            at, info, ring, last, early, order, head, theirs[last], own_rows, more_rows, right, left
        )
        sums, more_others, more_owns = tail(
            at, info, ring, order, head, mine, theirs, [*others, *owns], full, left, squares
        )
        others = dict(zip(order, [*others, *more_others]))
        owns = dict(zip(order, [*owns, *more_owns]))
        summed, sums = scatter_sum(owns, others, terms, sums, steps)
        vector, squares, ritz = update(at, info, vector, precond, sums, summed, ring)
        values.append(ritz[0, :1])
    for stage in steps:
        squares = stage_sum(squares, stage)
    return (vector * jnp.sqrt(cells / jnp.sum(squares)), jnp.concatenate(values))


def solution(mesh):
    return jax.shard_map(
        per_device,
        mesh=mesh,
        in_specs=(
            P("sector", "term", None),
            P("sector", "term", None),
            P("sector"),
            P(("sector", "term"), None, None),
            P(("sector", "term"), None, None),
            P(("sector", "term")),
            P(("sector", "term")),
            P(("sector", "term")),
        ),
        out_specs=(P("sector", "term", None), P()),
        check_vma=False,
    )
```

```python
import functools

import jax
import jax.numpy as jnp
from jax import lax
from jax.experimental import pallas as pl
from jax.experimental.pallas import tpu as pltpu
from jax.sharding import PartitionSpec as P

STEPS = 3
VMEM_LIMIT = 14 * 1024 * 1024
F32 = jnp.float32
BF16 = jnp.bfloat16


def split(value):
    high = value.astype(BF16)
    return high, (value - high.astype(F32)).astype(BF16)


def dot3(a_high, a_low, b_high, b_low):
    def dot(a, b):
        return jnp.dot(a, b, preferred_element_type=F32)

    return dot(a_high, b_high) + (dot(a_high, b_low) + dot(a_low, b_high))


def call(kernel, name, info, arrays, results, flops, scratch=()):
    held = pl.BlockSpec(memory_space=pltpu.VMEM)
    return pl.pallas_call(
        kernel,
        in_specs=[pl.BlockSpec(memory_space=pltpu.SMEM)] + [held] * len(arrays),
        out_specs=[held] * len(results),
        out_shape=[pltpu.VMEM(shape, dtype) for shape, dtype in results],
        scratch_shapes=list(scratch),
        compiler_params=pltpu.CompilerParams(vmem_limit_bytes=VMEM_LIMIT),
        cost_estimate=pl.CostEstimate(flops=flops, bytes_accessed=0, transcendentals=0),
        name=name,
    )(info, *arrays)


class Place:
    def __init__(self, slots):
        self.target, self.ring, self.side = slots, 2 * slots, 2 * slots + 1
        self.count, self.limits = 2 * slots + 2, 2 * slots + 3


def split_kernel(at, info, operator, *refs):
    high, low = refs[-2:]
    k = pl.program_id(0)

    @pl.when(k < info[at.count])
    def _():
        high[k], low[k] = split(operator[0])


def split_operators(info, operators, earlier, name):
    slots, width, _ = operators.shape
    at = Place(slots)
    return pl.pallas_call(
        functools.partial(split_kernel, at),
        grid_spec=pltpu.PrefetchScalarGridSpec(
            num_scalar_prefetch=1,
            grid=(slots - 1,),
            in_specs=[
                pl.BlockSpec(
                    (1, width, width), lambda k, info: (jnp.minimum(k, info[at.count] - 1), 0, 0)
                )
            ]
            + [pl.BlockSpec(memory_space=pltpu.VMEM)] * len(earlier),
            out_specs=[pl.BlockSpec(memory_space=pltpu.VMEM)] * 2,
        ),
        out_shape=[pltpu.VMEM((slots - 1, width, width), BF16)] * 2,
        compiler_params=pltpu.CompilerParams(vmem_limit_bytes=VMEM_LIMIT),
        cost_estimate=pl.CostEstimate(
            flops=0, bytes_accessed=slots * width * width * 4, transcendentals=0
        ),
        name=name,
    )(info, operators, *earlier)


def split_blocks(blocks, high, low):
    share = blocks[0].shape[1]
    for place, block in enumerate(blocks):
        rows = pl.ds(place * share, share)
        high[:, rows, :], low[:, rows, :] = split(block[...])


def lanes(value):
    total = jnp.sum(value, axis=tuple(range(value.ndim - 1)))[None]
    width = total.shape[1]
    return sum(total[:, c : c + 128] for c in range(0, width, 128))


def inner_kernel(at, ring, info, *refs):
    blocks = refs[:ring]
    right_high, right_low = refs[ring : ring + 2]
    out_high, out_low, token, high, low = refs[-5:]
    token[...] = jnp.zeros_like(token)
    split_blocks(blocks, high, low)

    def one(k, carry):
        source = info[k]
        out_high[k], out_low[k] = split(
            dot3(high[source], low[source], right_high[k], right_low[k])
        )
        return carry

    lax.fori_loop(0, info[at.count], one, 0)


def inner_rows(at, info, blocks, right, earlier=()):
    ring = len(blocks)
    live, width, _ = right[0].shape
    sectors, share, _ = blocks[0].shape
    rows = ring * share
    return call(
        functools.partial(inner_kernel, at, ring),
        "inner_rows",
        info,
        [*blocks, *right, *earlier],
        [((live, rows, width), BF16)] * 2 + [((1, 128), F32)],
        live * rows * width * width * 6,
        [pltpu.VMEM((sectors, rows, width), BF16)] * 2,
    )


def first_row(at, info, ring, share, offset, side):
    around = lax.rem(info[at.ring] + offset, ring)
    return pl.multiple_of((around * 2 + side) * share, share)


def outer_rows(at, info, k, ring, places, left, full, outs):
    share = outs[0].shape[1]
    picks = [pl.ds(first_row(at, info, ring, share, *place), share) for place in places]
    high, low = (
        jnp.concatenate([part[k, pick, :] for pick in picks], axis=0) for part in left
    )
    product = dot3(high, low, full[0][k], full[1][k])
    target = info[at.target + k]
    for i, out in enumerate(outs):
        out[target] += product[i * share : (i + 1) * share]


def middle_kernel(at, ring, last, groups, order, head, info, *refs):
    block, parts, refs = refs[0], refs[1 : 1 + 2 * len(groups)], refs[1 + 2 * len(groups) :]
    right_high, right_low, left_high, left_low = refs[:4]
    full_high, full_low = refs[4:6]
    outs, (high, low) = refs[6:-2], refs[-2:]
    share = block.shape[1]
    side = info[at.side]
    split_blocks([block], high, low)
    for out in outs:
        out[...] = jnp.zeros_like(out)
    places = [(r, 1 - side) for r in order[: head[0]]] + [(r, side) for r in order[: head[1]]]

    def put(out, k, r, other, value):
        rows = pl.ds(first_row(at, info, ring, share, r, 1 - side if other else side), share)
        out[k, rows, :] = value

    def one(k, carry):
        source = info[k]
        inner = split(dot3(high[source], low[source], right_high[k], right_low[k]))
        for which, out in enumerate((full_high, full_low)):
            for g, group in enumerate(groups):
                for i, (r, other) in enumerate(group):
                    put(out, k, r, other, parts[2 * g + which][k, i * share : (i + 1) * share, :])
            put(out, k, last, True, inner[which])
        outer_rows(
            at, info, k, ring, places, (left_high, left_low), (full_high, full_low), outs
        )
        return carry

    lax.fori_loop(0, info[at.count], one, 0)


def middle(at, info, ring, last, groups, order, head, block, parts, right, left):
    live, width, _ = right[0].shape
    sectors, share, _ = block.shape
    count = sum(head)
    results = call(
        functools.partial(middle_kernel, at, ring, last, groups, order, head),
        "middle",
        info,
        [block, *(array for part in parts for array in part), *right, *left],
        [((live, width, width), BF16)] * 2 + [(block.shape, F32)] * count,
        live * share * (1 + count) * width * width * 6,
        [pltpu.VMEM((sectors, share, width), BF16)] * 2,
    )
    return results[:2], results[2 : 2 + head[0]], results[2 + head[0] :]


def tail_kernel(at, ring, order, head, info, *refs):
    mine, theirs, refs = refs[:ring], refs[ring : 2 * ring], refs[2 * ring :]
    heads, refs = refs[: sum(head)], refs[sum(head) :]
    full_high, full_low, left_high, left_low, squares, sums = refs[:6]
    outs = refs[6:]
    side = info[at.side]
    for out in outs:
        out[...] = jnp.zeros_like(out)
    others, owns = order[head[0] :], order[head[1] :]
    places = [(r, 1 - side) for r in others] + [(r, side) for r in owns]

    def one(k, carry):
        outer_rows(
            at, info, k, ring, places, (left_high, left_low), (full_high, full_low), outs
        )
        return carry

    lax.fori_loop(0, info[at.count], one, 0)
    pairs = [(theirs[r], heads[i]) for i, r in enumerate(order[: head[0]])]
    pairs += [(mine[r], heads[head[0] + i]) for i, r in enumerate(order[: head[1]])]
    pairs += [(theirs[r], outs[i]) for i, r in enumerate(others)]
    pairs += [(mine[r], outs[len(others) + i]) for i, r in enumerate(owns)]
    dots = sum(lanes(block[...] * out[...]) for block, out in pairs)
    row = lax.broadcasted_iota(jnp.int32, sums.shape, 0)
    sums[...] = jnp.where(row == 0, dots, jnp.where(row == 1, squares[...], 0.0))


def tail(at, info, ring, order, head, mine, theirs, heads, full, left, squares):
    live, width, _ = left[0].shape
    share = mine[0].shape[1]
    count = 2 * ring - sum(head)
    results = call(
        functools.partial(tail_kernel, at, ring, order, head),
        "tail",
        info,
        [*mine, *theirs, *heads, *full, *left, squares],
        [((8, 128), F32)] + [(mine[0].shape, F32)] * count,
        0,
    )
    others = ring - head[0]
    return results[0], results[1 : 1 + others], results[1 + others :]


def inside(at, info, shape, ring):
    share = shape[1]
    start = (info[at.ring] * 2 + info[at.side]) * share
    rows = start + lax.broadcasted_iota(jnp.int32, shape[1:], 0)
    cols = lax.broadcasted_iota(jnp.int32, shape[1:], 1)
    return [
        ((rows < info[at.limits + s]) & (cols < info[at.limits + s])).astype(F32)
        for s in range(shape[0])
    ]


def begin_kernel(at, ring, info, trial, vector, squares):
    total = jnp.zeros(squares.shape, F32)
    for s, mask in enumerate(inside(at, info, trial.shape, ring)):
        value = mask * trial[s]
        vector[s] = value
        total = total + lanes(value * value)
    squares[...] = total


def begin(at, info, trial, ring):
    return call(
        functools.partial(begin_kernel, at, ring),
        "begin",
        info,
        [trial],
        [(trial.shape, F32), ((1, 128), F32)],
        trial.size * 4,
    )


def update_kernel(at, ring, info, *refs):
    vector, precond, refs = refs[0], refs[1], refs[2:]
    sums, terms, (result, squares, ritz) = refs[:ring], refs[ring:-3], refs[-3:]
    sums = [part[...] for part in sums]
    while len(sums) > 1:
        half = len(sums) // 2
        sums = [sums[r] + sums[r + half] for r in range(half)]
    both = jnp.sum(sums[0], axis=1, keepdims=True)
    theta = both[0:1] / both[1:2]
    ritz[...] = jnp.broadcast_to(theta, ritz.shape)
    total = jnp.zeros(squares.shape, F32)
    for s, mask in enumerate(inside(at, info, vector.shape, ring)):
        sig = mask * sum(term[s] for term in terms)
        value = vector[s] - (sig - theta * vector[s]) / precond[s]
        result[s] = value
        total = total + lanes(value * value)
    squares[...] = total


def update(at, info, vector, precond, sums, terms, ring):
    return call(
        functools.partial(update_kernel, at, ring),
        "update",
        info,
        [vector, precond, *sums, *terms],
        [(vector.shape, F32), ((1, 128), F32), ((1, 128), F32)],
        vector.size * 8,
    )


def across(value, terms):
    return lax.ppermute(value, "term", [(i, i ^ 1) for i in range(terms)])


def around(value, terms, shift):
    return lax.ppermute(value, "term", [(i, (i + 2 * shift) % terms) for i in range(terms)])


def stages(sectors, terms):
    inner = [("term", terms, 1)]
    across_sectors = [("sector", sectors, 1 << bit) for bit in range(sectors.bit_length() - 1)]
    outer = [("term", terms, 1 << bit) for bit in range(1, terms.bit_length() - 1)]
    return inner + across_sectors, outer


def stage_sum(values, stage):
    axis, size, step = stage
    return values + lax.ppermute(values, axis, [(i, i ^ step) for i in range(size)])


def send_order(ring):
    ups = ring // 2
    downs = ring - 1 - ups
    order = []
    for hop in range(ups, 0, -1):
        order.append(hop)
        if hop <= downs:
            order.append((ring - hop) % ring)
    return order + [0]


def scatter_sum(own, other, terms, sums, steps):
    ring = terms // 2
    ups = ring // 2
    downs = ring - 1 - ups
    received = {r: across(other[r], terms) for r in send_order(ring)}
    inner, *outer = steps
    sums = stage_sum(sums, inner)
    up = down = None
    for hop in range(ups, 0, -1):
        value = own[hop] + received[hop]
        value, sums = lax.optimization_barrier((value if up is None else value + up, sums))
        up = around(value, terms, 1)
        if hop == ups:
            for stage in outer:
                sums = stage_sum(sums, stage)
        if hop <= downs:
            back = (ring - hop) % ring
            value = own[back] + received[back]
            value, sums = lax.optimization_barrier((value if down is None else value + down, sums))
            down = around(value, terms, -1)
    parts = [sums] + [around(sums, terms, shift) for shift in range(1, ring)]
    return [term for term in (own[0], received[0], up, down) if term is not None], parts


def per_device(
    trial, precond, sector_dims, left_ops, right_ops, task_source, task_target, task_count
):
    sec_dev, share, width = trial.shape
    slots = left_ops.shape[0]
    sectors, terms = lax.axis_size("sector"), lax.axis_size("term")
    ring = terms // 2
    cells = float(sec_dev * sectors * width * width)
    term = lax.axis_index("term").astype(jnp.int32)
    at = Place(slots)
    info = jnp.concatenate(
        [task_source, task_target, jnp.stack([term // 2, term % 2]), task_count, sector_dims]
    )
    values = []
    vector, squares = begin(at, info, trial, ring)
    steps, outer_steps = stages(sectors, terms)
    order = send_order(ring)
    ups = ring // 2
    downs = ring - 1 - ups
    last = ring - ups
    head = (ring // 2, ring // 4)
    right = left = None
    for step in range(STEPS):
        mine, theirs, groups, parts = {0: vector}, {}, [], []
        token = None
        for hop in range(1, ups + 1):
            value = mine[(ring - hop + 1) % ring]
            if token is not None:
                value, token = lax.optimization_barrier((value, token))
                if step == 0 and hop == 2:
                    theirs[0], token = token, None
            mine[ring - hop] = around(value, terms, 1)
            fresh = [(ring - hop + 1) % ring]
            if hop <= downs:
                mine[hop] = around(mine[hop - 1], terms, -1)
            if hop > 1 and hop - 1 <= downs:
                fresh.append(hop - 1)
            for r in fresh:
                theirs[r] = across(mine[r], terms)
            if step == 0 and hop == 1:
                token = theirs[0]
                continue
            if step == 0 and hop == 2:
                arrived = [mine[ring - 1], mine[1]]
                right = split_operators(info, right_ops, arrived, "split_right")
                left = split_operators(info, left_ops, arrived, "split_left")
                group = [(0, False), (0, True)] + [(r, False) for r in fresh]
            elif hop == 1:
                group = [(0, False), (0, True)]
            else:
                group = [(r, False) for r in fresh] + before
            before = [(r, True) for r in fresh]
            if hop == 1:
                before = []
            *part, token = inner_rows(
                at,
                info,
                [(theirs if other else mine)[r] for r, other in group],
                right,
                () if token is None else (token,),
            )
            groups.append(group)
            parts.append(part)
        fresh = [last] + ([ups] if ups <= downs else [])
        for r in fresh:
            theirs[r] = across(mine[r], terms)
        group = [(r, False) for r in fresh] + before + [(r, True) for r in fresh if r != last]
        *part, token = inner_rows(
            at, info, [(theirs if other else mine)[r] for r, other in group], right, (token,)
        )
        groups.append(group)
        parts.append(part)
        full, others, owns = middle(
            at, info, ring, last, groups, order, head, theirs[last], parts, right, left
        )
        sums, more_others, more_owns = tail(
            at,
            info,
            ring,
            order,
            head,
            [mine[r] for r in range(ring)],
            [theirs[r] for r in range(ring)],
            [*others, *owns],
            full,
            left,
            squares,
        )
        others = dict(zip(order, [*others, *more_others]))
        owns = dict(zip(order, [*owns, *more_owns]))
        summed, sums = scatter_sum(owns, others, terms, sums, steps)
        vector, squares, ritz = update(at, info, vector, precond, sums, summed, ring)
        values.append(ritz[0, :1])
    for stage in steps + outer_steps:
        squares = stage_sum(squares, stage)
    return (vector * jnp.sqrt(cells / jnp.sum(squares)), jnp.concatenate(values))


def solution(mesh):
    return jax.shard_map(
        per_device,
        mesh=mesh,
        in_specs=(
            P("sector", "term", None),
            P("sector", "term", None),
            P("sector"),
            P(("sector", "term"), None, None),
            P(("sector", "term"), None, None),
            P(("sector", "term")),
            P(("sector", "term")),
            P(("sector", "term")),
        ),
        out_specs=(P("sector", "term", None), P()),
        check_vma=False,
    )
```

```python
import functools

import jax
import jax.numpy as jnp
from jax import lax
from jax.experimental import pallas as pl
from jax.experimental.pallas import tpu as pltpu
from jax.sharding import PartitionSpec as P

STEPS = 3
VMEM_LIMIT = 14 * 1024 * 1024
SPLIT_VMEM_LIMIT = 42 * 1024 * 1024
F32 = jnp.float32
BF16 = jnp.bfloat16


def split(value):
    high = value.astype(BF16)
    return high, (value - high.astype(F32)).astype(BF16)


def dot3(a_high, a_low, b_high, b_low):
    def dot(a, b):
        return jnp.dot(a, b, preferred_element_type=F32)

    return dot(a_high, b_high) + (dot(a_high, b_low) + dot(a_low, b_high))


def call(kernel, name, info, arrays, results, flops, scratch=()):
    held = pl.BlockSpec(memory_space=pltpu.VMEM)
    return pl.pallas_call(
        kernel,
        in_specs=[pl.BlockSpec(memory_space=pltpu.SMEM)] + [held] * len(arrays),
        out_specs=[held] * len(results),
        out_shape=[pltpu.VMEM(shape, dtype) for shape, dtype in results],
        scratch_shapes=list(scratch),
        compiler_params=pltpu.CompilerParams(vmem_limit_bytes=VMEM_LIMIT),
        cost_estimate=pl.CostEstimate(flops=flops, bytes_accessed=0, transcendentals=0),
        name=name,
    )(info, *arrays)


class Place:
    def __init__(self, slots):
        self.target, self.ring, self.side = slots, 2 * slots, 2 * slots + 1
        self.count, self.limits = 2 * slots + 2, 2 * slots + 3


def split_kernel(at, info, operator, *refs):
    high, low = refs[-2:]
    k = pl.program_id(0)

    @pl.when(k < info[at.count])
    def _():
        high[k], low[k] = split(operator[0])


def split_operators(info, operators, earlier, name):
    slots, width, _ = operators.shape
    at = Place(slots)
    return pl.pallas_call(
        functools.partial(split_kernel, at),
        grid_spec=pltpu.PrefetchScalarGridSpec(
            num_scalar_prefetch=1,
            grid=(slots - 1,),
            in_specs=[
                pl.BlockSpec(
                    (1, width, width), lambda k, info: (jnp.minimum(k, info[at.count] - 1), 0, 0)
                )
            ]
            + [pl.BlockSpec(memory_space=pltpu.VMEM)] * len(earlier),
            out_specs=[pl.BlockSpec(memory_space=pltpu.VMEM)] * 2,
        ),
        out_shape=[pltpu.VMEM((slots - 1, width, width), BF16)] * 2,
        compiler_params=pltpu.CompilerParams(vmem_limit_bytes=SPLIT_VMEM_LIMIT),
        cost_estimate=pl.CostEstimate(
            flops=0, bytes_accessed=slots * width * width * 4, transcendentals=0
        ),
        name=name,
    )(info, operators, *earlier)


def split_blocks(blocks, high, low):
    share = blocks[0].shape[1]
    for place, block in enumerate(blocks):
        rows = pl.ds(place * share, share)
        high[:, rows, :], low[:, rows, :] = split(block[...])


def lanes(value):
    total = jnp.sum(value, axis=tuple(range(value.ndim - 1)))[None]
    width = total.shape[1]
    return sum(total[:, c : c + 128] for c in range(0, width, 128))


def inner_kernel(at, ring, info, *refs):
    blocks = refs[:ring]
    right_high, right_low = refs[ring : ring + 2]
    out_high, out_low, token, high, low = refs[-5:]
    token[...] = jnp.zeros_like(token)
    split_blocks(blocks, high, low)

    def one(k, carry):
        source = info[k]
        out_high[k], out_low[k] = split(
            dot3(high[source], low[source], right_high[k], right_low[k])
        )
        return carry

    lax.fori_loop(0, info[at.count], one, 0)


def inner_rows(at, info, blocks, right, earlier=()):
    ring = len(blocks)
    live, width, _ = right[0].shape
    sectors, share, _ = blocks[0].shape
    rows = ring * share
    return call(
        functools.partial(inner_kernel, at, ring),
        "inner_rows",
        info,
        [*blocks, *right, *earlier],
        [((live, rows, width), BF16)] * 2 + [((1, 128), F32)],
        live * rows * width * width * 6,
        [pltpu.VMEM((sectors, rows, width), BF16)] * 2,
    )


def first_row(at, info, ring, share, offset, side):
    around = lax.rem(info[at.ring] + offset, ring)
    return pl.multiple_of((around * 2 + side) * share, share)


def outer_rows(at, info, k, ring, places, left, full, outs):
    share = outs[0].shape[1]
    picks = [pl.ds(first_row(at, info, ring, share, *place), share) for place in places]
    high, low = (
        jnp.concatenate([part[k, pick, :] for pick in picks], axis=0) for part in left
    )
    product = dot3(high, low, full[0][k], full[1][k])
    target = info[at.target + k]
    for i, out in enumerate(outs):
        out[target] += product[i * share : (i + 1) * share]


def middle_kernel(at, ring, lasts, groups, order, head, info, *refs):
    blocks, refs = refs[: len(lasts)], refs[len(lasts) :]
    parts, refs = refs[: 2 * len(groups)], refs[2 * len(groups) :]
    right_high, right_low, left_high, left_low = refs[:4]
    full_high, full_low = refs[4:6]
    outs, (high, low) = refs[6:-2], refs[-2:]
    share = blocks[0].shape[1]
    side = info[at.side]
    split_blocks(blocks, high, low)
    for out in outs:
        out[...] = jnp.zeros_like(out)
    places = [(r, 1 - side) for r in order[: head[0]]] + [(r, side) for r in order[: head[1]]]

    def put(out, k, r, other, value):
        rows = pl.ds(first_row(at, info, ring, share, r, 1 - side if other else side), share)
        out[k, rows, :] = value

    def one(k, carry):
        source = info[k]
        inner = split(dot3(high[source], low[source], right_high[k], right_low[k]))
        for which, out in enumerate((full_high, full_low)):
            for g, group in enumerate(groups):
                for i, (r, other) in enumerate(group):
                    put(out, k, r, other, parts[2 * g + which][k, i * share : (i + 1) * share, :])
            for i, r in enumerate(lasts):
                put(out, k, r, True, inner[which][i * share : (i + 1) * share])
        outer_rows(
            at, info, k, ring, places, (left_high, left_low), (full_high, full_low), outs
        )
        return carry

    lax.fori_loop(0, info[at.count], one, 0)


def middle(at, info, ring, lasts, groups, order, head, blocks, parts, right, left):
    live, width, _ = right[0].shape
    sectors, share, _ = blocks[0].shape
    count = sum(head)
    results = call(
        functools.partial(middle_kernel, at, ring, lasts, groups, order, head),
        "middle",
        info,
        [*blocks, *(array for part in parts for array in part), *right, *left],
        [((live, width, width), BF16)] * 2 + [(blocks[0].shape, F32)] * count,
        live * share * (len(lasts) + count) * width * width * 6,
        [pltpu.VMEM((sectors, len(lasts) * share, width), BF16)] * 2,
    )
    return results[:2], results[2 : 2 + head[0]], results[2 + head[0] :]


def tail_kernel(at, ring, order, head, info, *refs):
    mine, theirs, refs = refs[:ring], refs[ring : 2 * ring], refs[2 * ring :]
    heads, refs = refs[: sum(head)], refs[sum(head) :]
    full_high, full_low, left_high, left_low, squares, sums = refs[:6]
    outs = refs[6:]
    side = info[at.side]
    for out in outs:
        out[...] = jnp.zeros_like(out)
    others, owns = order[head[0] :], order[head[1] :]
    places = [(r, 1 - side) for r in others] + [(r, side) for r in owns]

    def one(k, carry):
        outer_rows(
            at, info, k, ring, places, (left_high, left_low), (full_high, full_low), outs
        )
        return carry

    lax.fori_loop(0, info[at.count], one, 0)
    pairs = [(theirs[r], heads[i]) for i, r in enumerate(order[: head[0]])]
    pairs += [(mine[r], heads[head[0] + i]) for i, r in enumerate(order[: head[1]])]
    pairs += [(theirs[r], outs[i]) for i, r in enumerate(others)]
    pairs += [(mine[r], outs[len(others) + i]) for i, r in enumerate(owns)]
    dots = sum(lanes(block[...] * out[...]) for block, out in pairs)
    row = lax.broadcasted_iota(jnp.int32, sums.shape, 0)
    sums[...] = jnp.where(row == 0, dots, jnp.where(row == 1, squares[...], 0.0))


def tail(at, info, ring, order, head, mine, theirs, heads, full, left, squares):
    live, width, _ = left[0].shape
    share = mine[0].shape[1]
    count = 2 * ring - sum(head)
    results = call(
        functools.partial(tail_kernel, at, ring, order, head),
        "tail",
        info,
        [*mine, *theirs, *heads, *full, *left, squares],
        [((8, 128), F32)] + [(mine[0].shape, F32)] * count,
        0,
    )
    others = ring - head[0]
    return results[0], results[1 : 1 + others], results[1 + others :]


def inside(at, info, shape, ring):
    share = shape[1]
    start = (info[at.ring] * 2 + info[at.side]) * share
    rows = start + lax.broadcasted_iota(jnp.int32, shape[1:], 0)
    cols = lax.broadcasted_iota(jnp.int32, shape[1:], 1)
    return [
        ((rows < info[at.limits + s]) & (cols < info[at.limits + s])).astype(F32)
        for s in range(shape[0])
    ]


def begin_kernel(at, ring, info, trial, vector, squares):
    total = jnp.zeros(squares.shape, F32)
    for s, mask in enumerate(inside(at, info, trial.shape, ring)):
        value = mask * trial[s]
        vector[s] = value
        total = total + lanes(value * value)
    squares[...] = total


def begin(at, info, trial, ring):
    return call(
        functools.partial(begin_kernel, at, ring),
        "begin",
        info,
        [trial],
        [(trial.shape, F32), ((1, 128), F32)],
        trial.size * 4,
    )


def update_kernel(at, ring, info, *refs):
    vector, precond, refs = refs[0], refs[1], refs[2:]
    sums, terms, (result, squares, ritz) = refs[:ring], refs[ring:-3], refs[-3:]
    sums = [part[...] for part in sums]
    while len(sums) > 1:
        half = len(sums) // 2
        sums = [sums[r] + sums[r + half] for r in range(half)]
    both = jnp.sum(sums[0], axis=1, keepdims=True)
    theta = both[0:1] / both[1:2]
    ritz[...] = jnp.broadcast_to(theta, ritz.shape)
    total = jnp.zeros(squares.shape, F32)
    for s, mask in enumerate(inside(at, info, vector.shape, ring)):
        sig = mask * sum(term[s] for term in terms)
        value = vector[s] - (sig - theta * vector[s]) / precond[s]
        result[s] = value
        total = total + lanes(value * value)
    squares[...] = total


def update(at, info, vector, precond, sums, terms, ring):
    return call(
        functools.partial(update_kernel, at, ring),
        "update",
        info,
        [vector, precond, *sums, *terms],
        [(vector.shape, F32), ((1, 128), F32), ((1, 128), F32)],
        vector.size * 8,
    )


def across(value, terms):
    return lax.ppermute(value, "term", [(i, i ^ 1) for i in range(terms)])


def around(value, terms, shift):
    return lax.ppermute(value, "term", [(i, (i + 2 * shift) % terms) for i in range(terms)])


def stages(sectors, terms):
    inner = [("term", terms, 1)]
    across_sectors = [("sector", sectors, 1 << bit) for bit in range(sectors.bit_length() - 1)]
    outer = [("term", terms, 1 << bit) for bit in range(1, terms.bit_length() - 1)]
    return inner + across_sectors, outer


def stage_sum(values, stage):
    axis, size, step = stage
    return values + lax.ppermute(values, axis, [(i, i ^ step) for i in range(size)])


def send_order(ring):
    ups = ring // 2
    downs = ring - 1 - ups
    order = []
    for hop in range(ups, 0, -1):
        if hop <= downs:
            order.append((ring - hop) % ring)
        order.append(hop)
    return order + [0]


def scatter_sum(own, other, terms, sums, steps):
    ring = terms // 2
    ups = ring // 2
    downs = ring - 1 - ups
    received = {r: across(other[r], terms) for r in send_order(ring)}
    inner, *outer = steps
    sums = stage_sum(sums, inner)
    up = down = None
    for hop in range(ups, 0, -1):
        value = own[hop] + received[hop]
        value, sums = lax.optimization_barrier((value if up is None else value + up, sums))
        up = around(value, terms, 1)
        if hop == ups:
            for stage in outer:
                sums = stage_sum(sums, stage)
        if hop <= downs:
            back = (ring - hop) % ring
            value = own[back] + received[back]
            down = around(value if down is None else value + down, terms, -1)
    parts = [sums] + [around(sums, terms, shift) for shift in range(1, ring)]
    return [term for term in (own[0], received[0], up, down) if term is not None], parts


def per_device(
    trial, precond, sector_dims, left_ops, right_ops, task_source, task_target, task_count
):
    sec_dev, share, width = trial.shape
    slots = left_ops.shape[0]
    sectors, terms = lax.axis_size("sector"), lax.axis_size("term")
    ring = terms // 2
    cells = float(sec_dev * sectors * width * width)
    term = lax.axis_index("term").astype(jnp.int32)
    at = Place(slots)
    info = jnp.concatenate(
        [task_source, task_target, jnp.stack([term // 2, term % 2]), task_count, sector_dims]
    )
    values = []
    vector, squares = begin(at, info, trial, ring)
    steps, outer_steps = stages(sectors, terms)
    order = send_order(ring)
    ups = ring // 2
    downs = ring - 1 - ups
    last = ring - ups
    head = (1, 0)
    right = left = None
    for step in range(STEPS):
        mine, theirs, groups, parts = {0: vector}, {}, [], []
        token = None
        for hop in range(1, ups + 1):
            value = mine[(ring - hop + 1) % ring]
            if token is not None:
                value, token = lax.optimization_barrier((value, token))
                if step == 0 and hop == 2:
                    theirs[0], token = token, None
            mine[ring - hop] = around(value, terms, 1)
            fresh = [(ring - hop + 1) % ring]
            if hop <= downs:
                mine[hop] = around(mine[hop - 1], terms, -1)
            if hop > 1 and hop - 1 <= downs:
                fresh.append(hop - 1)
            for r in fresh:
                theirs[r] = across(mine[r], terms)
            if step == 0 and hop == 1:
                token = theirs[0]
                continue
            if step == 0 and hop == 2:
                arrived = [mine[ring - 1], mine[1]]
                right = split_operators(info, right_ops, arrived, "split_right")
                left = split_operators(info, left_ops, arrived, "split_left")
                group = [(0, False), (0, True)] + [(r, False) for r in fresh]
            elif hop == 1:
                group = [(0, False), (0, True)]
            else:
                group = [(r, False) for r in fresh] + before
            before = [(r, True) for r in fresh]
            if hop == 1:
                before = []
            *part, token = inner_rows(
                at,
                info,
                [(theirs if other else mine)[r] for r, other in group],
                right,
                () if token is None else (token,),
            )
            groups.append(group)
            parts.append(part)
        fresh = [last] + ([ups] if ups <= downs else [])
        for r in fresh:
            theirs[r] = across(mine[r], terms)
        lasts = [r for r, _ in before[1:]] + fresh
        group = [(r, False) for r in fresh] + before[:1]
        *part, token = inner_rows(
            at, info, [(theirs if other else mine)[r] for r, other in group], right, (token,)
        )
        groups.append(group)
        parts.append(part)
        full, others, owns = middle(
            at, info, ring, lasts, groups, order, head, [theirs[r] for r in lasts], parts, right, left
        )
        sums, more_others, more_owns = tail(
            at,
            info,
            ring,
            order,
            head,
            [mine[r] for r in range(ring)],
            [theirs[r] for r in range(ring)],
            [*others, *owns],
            full,
            left,
            squares,
        )
        others = dict(zip(order, [*others, *more_others]))
        owns = dict(zip(order, [*owns, *more_owns]))
        summed, sums = scatter_sum(owns, others, terms, sums, steps)
        vector, squares, ritz = update(at, info, vector, precond, sums, summed, ring)
        values.append(ritz[0, :1])
    for stage in steps + outer_steps:
        squares = stage_sum(squares, stage)
    return (vector * jnp.sqrt(cells / jnp.sum(squares)), jnp.concatenate(values))


def solution(mesh):
    return jax.shard_map(
        per_device,
        mesh=mesh,
        in_specs=(
            P("sector", "term", None),
            P("sector", "term", None),
            P("sector"),
            P(("sector", "term"), None, None),
            P(("sector", "term"), None, None),
            P(("sector", "term")),
            P(("sector", "term")),
            P(("sector", "term")),
        ),
        out_specs=(P("sector", "term", None), P()),
        check_vma=False,
    )
```

```python
import functools

import jax
import jax.numpy as jnp
from jax import lax
from jax.experimental import pallas as pl
from jax.experimental.pallas import tpu as pltpu
from jax.sharding import PartitionSpec as P

STEPS = 3
VMEM_LIMIT = 14 * 1024 * 1024
SPLIT_VMEM_LIMIT = 46 * 1024 * 1024
F32 = jnp.float32
BF16 = jnp.bfloat16


def split(value):
    high = value.astype(BF16)
    return high, (value - high.astype(F32)).astype(BF16)


def dot3(a_high, a_low, b_high, b_low):
    def dot(a, b):
        return jnp.dot(a, b, preferred_element_type=F32)

    rows = a_high.shape[0]
    both = dot(jnp.concatenate([a_high, a_low], axis=0), b_high)
    return both[:rows] + (both[rows:] + dot(a_high, b_low))


def call(kernel, name, info, arrays, results, flops, scratch=()):
    held = pl.BlockSpec(memory_space=pltpu.VMEM)
    return pl.pallas_call(
        kernel,
        in_specs=[pl.BlockSpec(memory_space=pltpu.SMEM)] + [held] * len(arrays),
        out_specs=[held] * len(results),
        out_shape=[pltpu.VMEM(shape, dtype) for shape, dtype in results],
        scratch_shapes=list(scratch),
        compiler_params=pltpu.CompilerParams(vmem_limit_bytes=VMEM_LIMIT),
        cost_estimate=pl.CostEstimate(flops=flops, bytes_accessed=0, transcendentals=0),
        name=name,
    )(info, *arrays)


class Place:
    def __init__(self, slots):
        self.target, self.ring, self.side = slots, 2 * slots, 2 * slots + 1
        self.count, self.limits = 2 * slots + 2, 2 * slots + 3


def split_kernel(rights, lefts, *refs):
    results, held, ready = refs[:4], refs[4], refs[5]
    live = held.shape[1]

    def copy(which, k):
        source = (rights, lefts)[which]
        return pltpu.make_async_copy(source.at[k], held.at[which, k], ready.at[which, k])

    for which in range(2):
        for k in range(live):
            copy(which, k).start()
    for which in range(2):
        high, low = results[2 * which : 2 * which + 2]

        def one(k, carry):
            copy(which, k).wait()
            high[k], low[k] = split(held[which, k])
            return carry

        lax.fori_loop(0, live, one, 0)


def split_operators(rights, lefts):
    slots, width, _ = rights.shape
    shape = (slots - 1, width, width)
    parts = pl.pallas_call(
        split_kernel,
        in_specs=[pl.BlockSpec(memory_space=pltpu.HBM)] * 2,
        out_specs=[pl.BlockSpec(memory_space=pltpu.VMEM)] * 4,
        out_shape=[pltpu.VMEM(shape, BF16)] * 4,
        scratch_shapes=[pltpu.VMEM((2, *shape), F32), pltpu.SemaphoreType.DMA((2, slots - 1))],
        compiler_params=pltpu.CompilerParams(vmem_limit_bytes=SPLIT_VMEM_LIMIT),
        cost_estimate=pl.CostEstimate(flops=0, bytes_accessed=2 * rights.size * 4, transcendentals=0),
        name="split_operators",
    )(rights, lefts)
    return parts[:2], parts[2:]


def split_blocks(blocks, high, low):
    share = blocks[0].shape[1]
    for place, block in enumerate(blocks):
        rows = pl.ds(place * share, share)
        high[:, rows, :], low[:, rows, :] = split(block[...])


def lanes(value):
    total = jnp.sum(value, axis=tuple(range(value.ndim - 1)))[None]
    width = total.shape[1]
    return sum(total[:, c : c + 128] for c in range(0, width, 128))


def inner_kernel(at, ring, info, *refs):
    blocks = refs[:ring]
    right_high, right_low = refs[ring : ring + 2]
    out_high, out_low, token, high, low = refs[-5:]
    token[...] = jnp.zeros_like(token)
    split_blocks(blocks, high, low)

    def one(k, carry):
        source = info[k]
        out_high[k], out_low[k] = split(
            dot3(high[source], low[source], right_high[k], right_low[k])
        )
        return carry

    lax.fori_loop(0, info[at.count], one, 0)


def inner_rows(at, info, blocks, right, earlier=()):
    ring = len(blocks)
    live, width, _ = right[0].shape
    sectors, share, _ = blocks[0].shape
    rows = ring * share
    return call(
        functools.partial(inner_kernel, at, ring),
        "inner_rows",
        info,
        [*blocks, *right, *earlier],
        [((live, rows, width), BF16)] * 2 + [((1, 128), F32)],
        live * rows * width * width * 6,
        [pltpu.VMEM((sectors, rows, width), BF16)] * 2,
    )


def first_row(at, info, ring, share, offset, side):
    around = lax.rem(info[at.ring] + offset, ring)
    return pl.multiple_of((around * 2 + side) * share, share)


def outer_rows(at, info, k, ring, places, left, full, outs):
    share = outs[0].shape[1]
    picks = [pl.ds(first_row(at, info, ring, share, *place), share) for place in places]
    high, low = (
        jnp.concatenate([part[k, pick, :] for pick in picks], axis=0) for part in left
    )
    product = dot3(high, low, full[0][k], full[1][k])
    target = info[at.target + k]
    for i, out in enumerate(outs):
        out[target] += product[i * share : (i + 1) * share]


def middle_kernel(at, ring, lasts, groups, order, head, info, *refs):
    blocks, refs = refs[: len(lasts)], refs[len(lasts) :]
    parts, refs = refs[: 2 * len(groups)], refs[2 * len(groups) :]
    right_high, right_low, left_high, left_low = refs[:4]
    full_high, full_low = refs[4:6]
    outs, (high, low) = refs[6:-2], refs[-2:]
    share = blocks[0].shape[1]
    side = info[at.side]
    split_blocks(blocks, high, low)
    for out in outs:
        out[...] = jnp.zeros_like(out)
    places = [(r, 1 - side) for r in order[: head[0]]] + [(r, side) for r in order[: head[1]]]

    def put(out, k, r, other, value):
        rows = pl.ds(first_row(at, info, ring, share, r, 1 - side if other else side), share)
        out[k, rows, :] = value

    def one(k, carry):
        source = info[k]
        inner = split(dot3(high[source], low[source], right_high[k], right_low[k]))
        for which, out in enumerate((full_high, full_low)):
            for g, group in enumerate(groups):
                for i, (r, other) in enumerate(group):
                    put(out, k, r, other, parts[2 * g + which][k, i * share : (i + 1) * share, :])
            for i, r in enumerate(lasts):
                put(out, k, r, True, inner[which][i * share : (i + 1) * share])
        outer_rows(
            at, info, k, ring, places, (left_high, left_low), (full_high, full_low), outs
        )
        return carry

    lax.fori_loop(0, info[at.count], one, 0)


def middle(at, info, ring, lasts, groups, order, head, blocks, parts, right, left):
    live, width, _ = right[0].shape
    sectors, share, _ = blocks[0].shape
    count = sum(head)
    results = call(
        functools.partial(middle_kernel, at, ring, lasts, groups, order, head),
        "middle",
        info,
        [*blocks, *(array for part in parts for array in part), *right, *left],
        [((live, width, width), BF16)] * 2 + [(blocks[0].shape, F32)] * count,
        live * share * (len(lasts) + count) * width * width * 6,
        [pltpu.VMEM((sectors, len(lasts) * share, width), BF16)] * 2,
    )
    return results[:2], results[2 : 2 + head[0]], results[2 + head[0] :]


def outer_kernel(at, ring, wanted, counted, info, *refs):
    full_high, full_low, left_high, left_low = refs[:4]
    outs = refs[-len(wanted) :]
    side = info[at.side]
    for out in outs:
        out[...] = jnp.zeros_like(out)
    places = [(r, 1 - side if other else side) for r, other in wanted]

    def one(k, carry):
        outer_rows(
            at, info, k, ring, places, (left_high, left_low), (full_high, full_low), outs
        )
        return carry

    lax.fori_loop(0, info[at.count], one, 0)
    if counted:
        squares, sums = refs[4], refs[-len(wanted) - 1]
        blocks = refs[5 : 5 + 2 * ring]
        totals = [*refs[5 + 2 * ring : 5 + 4 * ring - len(wanted)], *outs]
        dots = sum(lanes(block[...] * total[...]) for block, total in zip(blocks, totals))
        row = lax.broadcasted_iota(jnp.int32, sums.shape, 0)
        sums[...] = jnp.where(row == 0, dots, jnp.where(row == 1, squares[...], 0.0))


def outer_blocks(at, info, ring, wanted, full, left, counted=()):
    live, width, _ = left[0].shape
    share = width // (2 * ring)
    sectors = info.shape[0] - at.limits
    extra = [counted[0], *counted[1], *counted[2]] if counted else []
    return call(
        functools.partial(outer_kernel, at, ring, wanted, bool(counted)),
        "outer_blocks",
        info,
        [*full, *left, *extra],
        ([((8, 128), F32)] if counted else []) + [((sectors, share, width), F32)] * len(wanted),
        0,
    )


def inside(limits, first, start, shape):
    rows = start + lax.broadcasted_iota(jnp.int32, shape[1:], 0)
    cols = lax.broadcasted_iota(jnp.int32, shape[1:], 1)
    return [
        ((rows < limits[first + s]) & (cols < limits[first + s])).astype(F32)
        for s in range(shape[0])
    ]


def begin_kernel(limits, trial, vector, squares):
    total = jnp.zeros(squares.shape, F32)
    start = lax.axis_index("term").astype(jnp.int32) * trial.shape[1]
    for s, mask in enumerate(inside(limits, 0, start, trial.shape)):
        value = mask * trial[s]
        vector[s] = value
        total = total + lanes(value * value)
    squares[...] = total


def begin(limits, trial):
    return call(
        begin_kernel,
        "begin",
        limits,
        [trial],
        [(trial.shape, F32), ((1, 128), F32)],
        trial.size * 4,
    )


def update_kernel(at, ring, info, *refs):
    vector, precond, refs = refs[0], refs[1], refs[2:]
    sums, terms, (result, squares, ritz) = refs[:ring], refs[ring:-3], refs[-3:]
    sums = [part[...] for part in sums]
    while len(sums) > 1:
        half = len(sums) // 2
        sums = [sums[r] + sums[r + half] for r in range(half)]
    both = jnp.sum(sums[0], axis=1, keepdims=True)
    theta = both[0:1] / both[1:2]
    ritz[...] = jnp.broadcast_to(theta, ritz.shape)
    total = jnp.zeros(squares.shape, F32)
    start = (info[at.ring] * 2 + info[at.side]) * vector.shape[1]
    for s, mask in enumerate(inside(info, at.limits, start, vector.shape)):
        sig = mask * sum(term[s] for term in terms)
        value = vector[s] - (sig - theta * vector[s]) / precond[s]
        result[s] = value
        total = total + lanes(value * value)
    squares[...] = total


def update(at, info, vector, precond, sums, terms, ring):
    return call(
        functools.partial(update_kernel, at, ring),
        "update",
        info,
        [vector, precond, *sums, *terms],
        [(vector.shape, F32), ((1, 128), F32), ((1, 128), F32)],
        vector.size * 8,
    )


def across(value, terms):
    return lax.ppermute(value, "term", [(i, i ^ 1) for i in range(terms)])


def around(value, terms, shift):
    return lax.ppermute(value, "term", [(i, (i + 2 * shift) % terms) for i in range(terms)])


def stages(sectors, terms):
    inner = [("term", terms, 1)]
    across_sectors = [("sector", sectors, 1 << bit) for bit in range(sectors.bit_length() - 1)]
    outer = [("term", terms, 1 << bit) for bit in range(1, terms.bit_length() - 1)]
    return inner + across_sectors, outer


def stage_sum(values, stage):
    axis, size, step = stage
    return values + lax.ppermute(values, axis, [(i, i ^ step) for i in range(size)])


def send_order(ring):
    ups = ring // 2
    downs = ring - 1 - ups
    order = []
    for hop in range(ups, 0, -1):
        if hop <= downs:
            order.append((ring - hop) % ring)
        order.append(hop)
    return order + [0]


def scatter_sum(own, other, terms, sums, steps):
    ring = terms // 2
    ups = ring // 2
    downs = ring - 1 - ups
    received = {r: across(other[r], terms) for r in send_order(ring)}
    inner, *outer = steps
    sums = stage_sum(sums, inner)
    up = down = None
    for hop in range(ups, 0, -1):
        value = own[hop] + received[hop]
        if up is not None:
            value, sums = lax.optimization_barrier((value + up, sums))
        up = around(value, terms, 1)
        if hop <= downs:
            back = (ring - hop) % ring
            value = own[back] + received[back]
            down = around(value if down is None else value + down, terms, -1)
    for stage in outer:
        sums = stage_sum(sums, stage)
    parts = [sums] + [around(sums, terms, shift) for shift in range(1, ring)]
    return [term for term in (own[0], received[0], up, down) if term is not None], parts


def per_device(
    trial, precond, sector_dims, left_ops, right_ops, task_source, task_target, task_count
):
    sec_dev, share, width = trial.shape
    slots = left_ops.shape[0]
    sectors, terms = lax.axis_size("sector"), lax.axis_size("term")
    ring = terms // 2
    cells = float(sec_dev * sectors * width * width)
    term = lax.axis_index("term").astype(jnp.int32)
    at = Place(slots)
    info = jnp.concatenate(
        [task_source, task_target, jnp.stack([term // 2, term % 2]), task_count, sector_dims]
    )
    values = []
    vector, squares = begin(sector_dims, trial)
    steps, outer_steps = stages(sectors, terms)
    order = send_order(ring)
    ups = ring // 2
    downs = ring - 1 - ups
    last = ring - ups
    head = (1, 0)
    right, left = split_operators(right_ops, left_ops)
    for step in range(STEPS):
        mine, theirs, groups, parts = {0: vector}, {}, [], []
        token = None
        for hop in range(1, ups + 1):
            value = mine[(ring - hop + 1) % ring]
            if token is not None:
                value, token = lax.optimization_barrier((value, token))
            mine[ring - hop] = around(value, terms, 1)
            fresh = [(ring - hop + 1) % ring]
            if hop <= downs:
                mine[hop] = around(mine[hop - 1], terms, -1)
            if hop > 1 and hop - 1 <= downs:
                fresh.append(hop - 1)
            for r in fresh:
                theirs[r] = across(mine[r], terms)
            if hop == 1:
                group = [(0, False), (0, True)]
            else:
                group = [(r, False) for r in fresh] + before
            before = [(r, True) for r in fresh]
            if hop == 1:
                before = []
            *part, token = inner_rows(
                at,
                info,
                [(theirs if other else mine)[r] for r, other in group],
                right,
                () if token is None else (token,),
            )
            groups.append(group)
            parts.append(part)
        fresh = [last] + ([ups] if ups <= downs else [])
        for r in fresh:
            theirs[r] = across(mine[r], terms)
        lasts = [r for r, _ in before[1:]] + fresh
        group = [(r, False) for r in fresh] + before[:1]
        *part, token = inner_rows(
            at, info, [(theirs if other else mine)[r] for r, other in group], right, (token,)
        )
        groups.append(group)
        parts.append(part)
        full, others, _ = middle(
            at, info, ring, lasts, groups, order, head, [theirs[r] for r in lasts], parts, right, left
        )
        done = [(r, True) for r in order[:1]]
        totals = dict(zip(done, others))
        first = [(order[0], False)] + [(r, True) for r in order[1:-1]]
        totals.update(zip(first, outer_blocks(at, info, ring, first, full, left)))
        done += first
        rest = [(r, False) for r in order[1:]] + [(r, True) for r in order[-1:]]
        blocks = [(theirs if other else mine)[r] for r, other in done + rest]
        sums, *outs = outer_blocks(
            at, info, ring, rest, full, left, (squares, blocks, [totals[key] for key in done])
        )
        totals.update(zip(rest, outs))
        owns = {r: totals[r, False] for r in range(ring)}
        others = {r: totals[r, True] for r in range(ring)}
        summed, sums = scatter_sum(owns, others, terms, sums, steps)
        vector, squares, ritz = update(at, info, vector, precond, sums, summed, ring)
        values.append(ritz[0, :1])
    for stage in steps + outer_steps:
        squares = stage_sum(squares, stage)
    return (vector * jnp.sqrt(cells / jnp.sum(squares)), jnp.concatenate(values))


def solution(mesh):
    return jax.shard_map(
        per_device,
        mesh=mesh,
        in_specs=(
            P("sector", "term", None),
            P("sector", "term", None),
            P("sector"),
            P(("sector", "term"), None, None),
            P(("sector", "term"), None, None),
            P(("sector", "term")),
            P(("sector", "term")),
            P(("sector", "term")),
        ),
        out_specs=(P("sector", "term", None), P()),
        check_vma=False,
    )
```

```python
import functools

import jax
import jax.numpy as jnp
from jax import lax
from jax.experimental import pallas as pl
from jax.experimental.pallas import tpu as pltpu
from jax.sharding import PartitionSpec as P

STEPS = 3
VMEM_LIMIT = 14 * 1024 * 1024
SPLIT_VMEM_LIMIT = 41 * 1024 * 1024
F32 = jnp.float32
BF16 = jnp.bfloat16


def split(value):
    high = value.astype(BF16)
    return high, (value - high.astype(F32)).astype(BF16)


def dot3(a_high, a_low, b_high, b_low):
    def dot(a, b):
        return jnp.dot(a, b, preferred_element_type=F32)

    rows = a_high.shape[0]
    both = dot(jnp.concatenate([a_high, a_low], axis=0), b_high)
    return both[:rows] + (both[rows:] + dot(a_high, b_low))


def call(kernel, name, info, arrays, results, flops, scratch=()):
    held = pl.BlockSpec(memory_space=pltpu.VMEM)
    return pl.pallas_call(
        kernel,
        in_specs=[pl.BlockSpec(memory_space=pltpu.SMEM)] + [held] * len(arrays),
        out_specs=[held] * len(results),
        out_shape=[pltpu.VMEM(shape, dtype) for shape, dtype in results],
        scratch_shapes=list(scratch),
        compiler_params=pltpu.CompilerParams(vmem_limit_bytes=VMEM_LIMIT),
        cost_estimate=pl.CostEstimate(flops=flops, bytes_accessed=0, transcendentals=0),
        name=name,
    )(info, *arrays)


class Place:
    def __init__(self, slots):
        self.target, self.ring, self.side = slots, 2 * slots, 2 * slots + 1
        self.count, self.limits = 2 * slots + 2, 2 * slots + 3


def split_kernel(rights, lefts, *refs):
    results, held, ready = refs[:4], refs[4], refs[5]
    live = held.shape[1]

    def copy(which, k):
        source = (rights, lefts)[which]
        return pltpu.make_async_copy(source.at[k], held.at[which, k], ready.at[which, k])

    for which in range(2):
        for k in range(live):
            copy(which, k).start()
    for which in range(2):
        high, low = results[2 * which : 2 * which + 2]

        def one(k, carry):
            copy(which, k).wait()
            high[k], low[k] = split(held[which, k])
            return carry

        lax.fori_loop(0, live, one, 0)


def split_operators(rights, lefts):
    slots, width, _ = rights.shape
    shape = (slots - 1, width, width)
    parts = pl.pallas_call(
        split_kernel,
        in_specs=[pl.BlockSpec(memory_space=pltpu.HBM)] * 2,
        out_specs=[pl.BlockSpec(memory_space=pltpu.VMEM)] * 4,
        out_shape=[pltpu.VMEM(shape, BF16)] * 4,
        scratch_shapes=[pltpu.VMEM((2, *shape), F32), pltpu.SemaphoreType.DMA((2, slots - 1))],
        compiler_params=pltpu.CompilerParams(vmem_limit_bytes=SPLIT_VMEM_LIMIT),
        cost_estimate=pl.CostEstimate(flops=0, bytes_accessed=2 * rights.size * 4, transcendentals=0),
        name="split_operators",
    )(rights, lefts)
    return parts[:2], parts[2:]


def split_blocks(blocks, high, low):
    share = blocks[0].shape[1]
    for place, block in enumerate(blocks):
        rows = pl.ds(place * share, share)
        high[:, rows, :], low[:, rows, :] = split(block[...])


def lanes(value):
    total = jnp.sum(value, axis=tuple(range(value.ndim - 1)))[None]
    width = total.shape[1]
    return sum(total[:, c : c + 128] for c in range(0, width, 128))


def inner_kernel(at, ring, info, *refs):
    blocks = refs[:ring]
    right_high, right_low = refs[ring : ring + 2]
    out_high, out_low, token, high, low = refs[-5:]
    token[...] = jnp.zeros_like(token)
    split_blocks(blocks, high, low)

    def one(k, carry):
        source = info[k]
        out_high[k], out_low[k] = split(
            dot3(high[source], low[source], right_high[k], right_low[k])
        )
        return carry

    lax.fori_loop(0, info[at.count], one, 0)


def inner_rows(at, info, blocks, right, earlier=()):
    ring = len(blocks)
    live, width, _ = right[0].shape
    sectors, share, _ = blocks[0].shape
    rows = ring * share
    return call(
        functools.partial(inner_kernel, at, ring),
        "inner_rows",
        info,
        [*blocks, *right, *earlier],
        [((live, rows, width), BF16)] * 2 + [((1, 128), F32)],
        live * rows * width * width * 6,
        [pltpu.VMEM((sectors, rows, width), BF16)] * 2,
    )


def first_row(at, info, ring, share, offset, side):
    around = lax.rem(info[at.ring] + offset, ring)
    return pl.multiple_of((around * 2 + side) * share, share)


def outer_rows(at, info, k, ring, places, left, full, outs):
    share = outs[0].shape[1]
    picks = [pl.ds(first_row(at, info, ring, share, *place), share) for place in places]
    high, low = (
        jnp.concatenate([part[k, pick, :] for pick in picks], axis=0) for part in left
    )
    product = dot3(high, low, full[0][k], full[1][k])
    target = info[at.target + k]
    for i, out in enumerate(outs):
        out[target] += product[i * share : (i + 1) * share]


def middle_kernel(at, ring, lasts, groups, order, head, info, *refs):
    blocks, refs = refs[: len(lasts)], refs[len(lasts) :]
    parts, refs = refs[: 2 * len(groups)], refs[2 * len(groups) :]
    right_high, right_low, left_high, left_low = refs[:4]
    full_high, full_low = refs[4:6]
    outs, (high, low) = refs[6:-2], refs[-2:]
    share = blocks[0].shape[1]
    side = info[at.side]
    split_blocks(blocks, high, low)
    for out in outs:
        out[...] = jnp.zeros_like(out)
    places = [(r, 1 - side) for r in order[: head[0]]] + [(r, side) for r in order[: head[1]]]

    def put(out, k, r, other, value):
        rows = pl.ds(first_row(at, info, ring, share, r, 1 - side if other else side), share)
        out[k, rows, :] = value

    def one(k, carry):
        source = info[k]
        inner = split(dot3(high[source], low[source], right_high[k], right_low[k]))
        for which, out in enumerate((full_high, full_low)):
            for g, group in enumerate(groups):
                for i, (r, other) in enumerate(group):
                    put(out, k, r, other, parts[2 * g + which][k, i * share : (i + 1) * share, :])
            for i, r in enumerate(lasts):
                put(out, k, r, True, inner[which][i * share : (i + 1) * share])
        outer_rows(
            at, info, k, ring, places, (left_high, left_low), (full_high, full_low), outs
        )
        return carry

    lax.fori_loop(0, info[at.count], one, 0)


def middle(at, info, ring, lasts, groups, order, head, blocks, parts, right, left):
    live, width, _ = right[0].shape
    sectors, share, _ = blocks[0].shape
    count = sum(head)
    results = call(
        functools.partial(middle_kernel, at, ring, lasts, groups, order, head),
        "middle",
        info,
        [*blocks, *(array for part in parts for array in part), *right, *left],
        [((live, width, width), BF16)] * 2 + [(blocks[0].shape, F32)] * count,
        live * share * (len(lasts) + count) * width * width * 6,
        [pltpu.VMEM((sectors, len(lasts) * share, width), BF16)] * 2,
    )
    return results[:2], results[2 : 2 + head[0]], results[2 + head[0] :]


def outer_kernel(at, ring, wanted, counted, info, *refs):
    full_high, full_low, left_high, left_low = refs[:4]
    outs = refs[-len(wanted) :]
    side = info[at.side]
    for out in outs:
        out[...] = jnp.zeros_like(out)
    places = [(r, 1 - side if other else side) for r, other in wanted]

    def one(k, carry):
        outer_rows(
            at, info, k, ring, places, (left_high, left_low), (full_high, full_low), outs
        )
        return carry

    lax.fori_loop(0, info[at.count], one, 0)
    if counted:
        squares, sums = refs[4], refs[-len(wanted) - 1]
        blocks = refs[5 : 5 + 2 * ring]
        totals = [*refs[5 + 2 * ring : 5 + 4 * ring - len(wanted)], *outs]
        dots = sum(lanes(block[...] * total[...]) for block, total in zip(blocks, totals))
        row = lax.broadcasted_iota(jnp.int32, sums.shape, 0)
        sums[...] = jnp.where(row == 0, dots, jnp.where(row == 1, squares[...], 0.0))


def outer_blocks(at, info, ring, wanted, full, left, counted=()):
    live, width, _ = left[0].shape
    share = width // (2 * ring)
    sectors = info.shape[0] - at.limits
    extra = [counted[0], *counted[1], *counted[2]] if counted else []
    return call(
        functools.partial(outer_kernel, at, ring, wanted, bool(counted)),
        "outer_blocks",
        info,
        [*full, *left, *extra],
        ([((8, 128), F32)] if counted else []) + [((sectors, share, width), F32)] * len(wanted),
        0,
    )


def inside(limits, first, start, shape):
    rows = start + lax.broadcasted_iota(jnp.int32, shape[1:], 0)
    cols = lax.broadcasted_iota(jnp.int32, shape[1:], 1)
    return [
        ((rows < limits[first + s]) & (cols < limits[first + s])).astype(F32)
        for s in range(shape[0])
    ]


def begin_kernel(limits, trial, vector, squares):
    total = jnp.zeros(squares.shape, F32)
    start = lax.axis_index("term").astype(jnp.int32) * trial.shape[1]
    for s, mask in enumerate(inside(limits, 0, start, trial.shape)):
        value = mask * trial[s]
        vector[s] = value
        total = total + lanes(value * value)
    squares[...] = total


def begin(limits, trial):
    return call(
        begin_kernel,
        "begin",
        limits,
        [trial],
        [(trial.shape, F32), ((1, 128), F32)],
        trial.size * 4,
    )


def update_kernel(at, ring, info, *refs):
    vector, precond, refs = refs[0], refs[1], refs[2:]
    sums, terms, (result, squares, ritz) = refs[:ring], refs[ring:-3], refs[-3:]
    sums = [part[...] for part in sums]
    while len(sums) > 1:
        half = len(sums) // 2
        sums = [sums[r] + sums[r + half] for r in range(half)]
    both = jnp.sum(sums[0], axis=1, keepdims=True)
    theta = both[0:1] / both[1:2]
    ritz[...] = jnp.broadcast_to(theta, ritz.shape)
    total = jnp.zeros(squares.shape, F32)
    start = (info[at.ring] * 2 + info[at.side]) * vector.shape[1]
    for s, mask in enumerate(inside(info, at.limits, start, vector.shape)):
        sig = mask * sum(term[s] for term in terms)
        value = vector[s] - (sig - theta * vector[s]) / precond[s]
        result[s] = value
        total = total + lanes(value * value)
    squares[...] = total


def update(at, info, vector, precond, sums, terms, ring):
    return call(
        functools.partial(update_kernel, at, ring),
        "update",
        info,
        [vector, precond, *sums, *terms],
        [(vector.shape, F32), ((1, 128), F32), ((1, 128), F32)],
        vector.size * 8,
    )


def across(value, terms):
    return lax.ppermute(value, "term", [(i, i ^ 1) for i in range(terms)])


def around(value, terms, shift):
    return lax.ppermute(value, "term", [(i, (i + 2 * shift) % terms) for i in range(terms)])


def stages(sectors, terms):
    inner = [("term", terms, 1)]
    across_sectors = [("sector", sectors, 1 << bit) for bit in range(sectors.bit_length() - 1)]
    outer = [("term", terms, 1 << bit) for bit in range(1, terms.bit_length() - 1)]
    return inner + across_sectors, outer


def stage_sum(values, stage):
    axis, size, step = stage
    return values + lax.ppermute(values, axis, [(i, i ^ step) for i in range(size)])


def send_order(ring):
    ups = ring // 2
    downs = ring - 1 - ups
    order = []
    for hop in range(ups, 0, -1):
        order.append(hop)
        if hop <= downs:
            order.append((ring - hop) % ring)
    return order + [0]


def scatter_sum(own, other, terms, sums, steps):
    ring = terms // 2
    ups = ring // 2
    downs = ring - 1 - ups
    received = {r: across(other[r], terms) for r in send_order(ring)}
    inner, *outer = steps
    sums = stage_sum(sums, inner)
    up = down = None
    for hop in range(ups, 0, -1):
        value = own[hop] + received[hop]
        value, sums = lax.optimization_barrier((value if up is None else value + up, sums))
        up = around(value, terms, 1)
        if hop == ups:
            for stage in outer:
                sums = stage_sum(sums, stage)
        if hop <= downs:
            back = (ring - hop) % ring
            value = own[back] + received[back]
            value, sums = lax.optimization_barrier((value if down is None else value + down, sums))
            down = around(value, terms, -1)
    parts = [sums] + [around(sums, terms, shift) for shift in range(1, ring)]
    return [term for term in (own[0], received[0], up, down) if term is not None], parts


def per_device(
    trial, precond, sector_dims, left_ops, right_ops, task_source, task_target, task_count
):
    sec_dev, share, width = trial.shape
    slots = left_ops.shape[0]
    sectors, terms = lax.axis_size("sector"), lax.axis_size("term")
    ring = terms // 2
    cells = float(sec_dev * sectors * width * width)
    term = lax.axis_index("term").astype(jnp.int32)
    at = Place(slots)
    info = jnp.concatenate(
        [task_source, task_target, jnp.stack([term // 2, term % 2]), task_count, sector_dims]
    )
    values = []
    vector, squares = begin(sector_dims, trial)
    steps, outer_steps = stages(sectors, terms)
    order = send_order(ring)
    ups = ring // 2
    downs = ring - 1 - ups
    last = ring - ups
    head = (ring // 2, ring // 4)
    right, left = split_operators(right_ops, left_ops)
    for step in range(STEPS):
        mine, theirs, groups, parts = {0: vector}, {}, [], []
        token = None
        for hop in range(1, ups + 1):
            value = mine[(ring - hop + 1) % ring]
            if token is not None:
                value, token = lax.optimization_barrier((value, token))
            mine[ring - hop] = around(value, terms, 1)
            fresh = [(ring - hop + 1) % ring]
            if hop <= downs:
                mine[hop] = around(mine[hop - 1], terms, -1)
            if hop > 1 and hop - 1 <= downs:
                fresh.append(hop - 1)
            for r in fresh:
                theirs[r] = across(mine[r], terms)
            if hop == 1:
                group = [(0, False), (0, True)]
            else:
                group = [(r, False) for r in fresh] + before
            before = [(r, True) for r in fresh]
            if hop == 1:
                before = []
            *part, token = inner_rows(
                at,
                info,
                [(theirs if other else mine)[r] for r, other in group],
                right,
                () if token is None else (token,),
            )
            groups.append(group)
            parts.append(part)
        fresh = [last] + ([ups] if ups <= downs else [])
        for r in fresh:
            theirs[r] = across(mine[r], terms)
        lasts = [r for r, _ in before[1:]] + fresh
        group = [(r, False) for r in fresh] + before[:1]
        *part, token = inner_rows(
            at, info, [(theirs if other else mine)[r] for r, other in group], right, (token,)
        )
        groups.append(group)
        parts.append(part)
        full, others, owns = middle(
            at, info, ring, lasts, groups, order, head, [theirs[r] for r in lasts], parts, right, left
        )
        done = [(r, True) for r in order[: head[0]]] + [(r, False) for r in order[: head[1]]]
        totals = dict(zip(done, [*others, *owns]))
        rest = [(r, True) for r in order[head[0] :]] + [(r, False) for r in order[head[1] :]]
        blocks = [(theirs if other else mine)[r] for r, other in done + rest]
        sums, *outs = outer_blocks(
            at, info, ring, rest, full, left, (squares, blocks, [totals[key] for key in done])
        )
        totals.update(zip(rest, outs))
        owns = {r: totals[r, False] for r in range(ring)}
        others = {r: totals[r, True] for r in range(ring)}
        summed, sums = scatter_sum(owns, others, terms, sums, steps)
        vector, squares, ritz = update(at, info, vector, precond, sums, summed, ring)
        values.append(ritz[0, :1])
    for stage in steps + outer_steps:
        squares = stage_sum(squares, stage)
    return (vector * jnp.sqrt(cells / jnp.sum(squares)), jnp.concatenate(values))


def solution(mesh):
    return jax.shard_map(
        per_device,
        mesh=mesh,
        in_specs=(
            P("sector", "term", None),
            P("sector", "term", None),
            P("sector"),
            P(("sector", "term"), None, None),
            P(("sector", "term"), None, None),
            P(("sector", "term")),
            P(("sector", "term")),
            P(("sector", "term")),
        ),
        out_specs=(P("sector", "term", None), P()),
        check_vma=False,
    )
```

```python
import functools

import jax
import jax.numpy as jnp
from jax import lax
from jax.experimental import pallas as pl
from jax.experimental.pallas import tpu as pltpu
from jax.sharding import PartitionSpec as P

STEPS = 3
VMEM_LIMIT = 14 * 1024 * 1024
SPLIT_VMEM_LIMIT = 20 * 1024 * 1024
F32 = jnp.float32
BF16 = jnp.bfloat16


def split(value):
    high = value.astype(BF16)
    return high, (value - high.astype(F32)).astype(BF16)


def dot3(a_high, a_low, b_high, b_low):
    def dot(a, b):
        return jnp.dot(a, b, preferred_element_type=F32)

    rows = a_high.shape[0]
    both = dot(jnp.concatenate([a_high, a_low], axis=0), b_high)
    return both[:rows] + (both[rows:] + dot(a_high, b_low))


def call(kernel, name, info, arrays, results, flops, scratch=()):
    held = pl.BlockSpec(memory_space=pltpu.VMEM)
    return pl.pallas_call(
        kernel,
        in_specs=[pl.BlockSpec(memory_space=pltpu.SMEM)] + [held] * len(arrays),
        out_specs=[held] * len(results),
        out_shape=[pltpu.VMEM(shape, dtype) for shape, dtype in results],
        scratch_shapes=list(scratch),
        compiler_params=pltpu.CompilerParams(vmem_limit_bytes=VMEM_LIMIT),
        cost_estimate=pl.CostEstimate(flops=flops, bytes_accessed=0, transcendentals=0),
        name=name,
    )(info, *arrays)


class Place:
    def __init__(self, slots):
        self.target, self.ring, self.side = slots, 2 * slots, 2 * slots + 1
        self.count, self.limits = 2 * slots + 2, 2 * slots + 3


def split_kernel(rights, lefts, *refs):
    results, held, ready = refs[:4], refs[4], refs[5]
    live = held.shape[1]

    def copy(which, k):
        source = (rights, lefts)[which]
        return pltpu.make_async_copy(source.at[k], held.at[which, k], ready.at[which, k])

    for which in range(2):
        for k in range(live):
            copy(which, k).start()
    for which in range(2):
        high, low = results[2 * which : 2 * which + 2]

        def one(k, carry):
            copy(which, k).wait()
            high[k], low[k] = split(held[which, k])
            return carry

        lax.fori_loop(0, live, one, 0)


def split_operators(rights, lefts):
    slots, width, _ = rights.shape
    shape = (slots - 1, width, width)
    parts = pl.pallas_call(
        split_kernel,
        in_specs=[pl.BlockSpec(memory_space=pltpu.HBM)] * 2,
        out_specs=[pl.BlockSpec(memory_space=pltpu.VMEM)] * 4,
        out_shape=[pltpu.VMEM(shape, BF16)] * 4,
        scratch_shapes=[pltpu.VMEM((2, *shape), F32), pltpu.SemaphoreType.DMA((2, slots - 1))],
        compiler_params=pltpu.CompilerParams(vmem_limit_bytes=SPLIT_VMEM_LIMIT),
        cost_estimate=pl.CostEstimate(flops=0, bytes_accessed=2 * rights.size * 4, transcendentals=0),
        name="split_operators",
    )(*(pltpu.with_memory_space_constraint(array, pltpu.HBM) for array in (rights, lefts)))
    return parts[:2], parts[2:]


def split_blocks(blocks, high, low):
    share = blocks[0].shape[1]
    for place, block in enumerate(blocks):
        rows = pl.ds(place * share, share)
        high[:, rows, :], low[:, rows, :] = split(block[...])


def lanes(value):
    total = jnp.sum(value, axis=tuple(range(value.ndim - 1)))[None]
    width = total.shape[1]
    return sum(total[:, c : c + 128] for c in range(0, width, 128))


def inner_kernel(at, ring, info, *refs):
    blocks = refs[:ring]
    right_high, right_low = refs[ring : ring + 2]
    out_high, out_low, token, high, low = refs[-5:]
    token[...] = jnp.zeros_like(token)
    split_blocks(blocks, high, low)

    def one(k, carry):
        source = info[k]
        out_high[k], out_low[k] = split(
            dot3(high[source], low[source], right_high[k], right_low[k])
        )
        return carry

    lax.fori_loop(0, info[at.count], one, 0)


def inner_rows(at, info, blocks, right, earlier=()):
    ring = len(blocks)
    live, width, _ = right[0].shape
    sectors, share, _ = blocks[0].shape
    rows = ring * share
    return call(
        functools.partial(inner_kernel, at, ring),
        "inner_rows",
        info,
        [*blocks, *right, *earlier],
        [((live, rows, width), BF16)] * 2 + [((1, 128), F32)],
        live * rows * width * width * 6,
        [pltpu.VMEM((sectors, rows, width), BF16)] * 2,
    )


def first_row(at, info, ring, share, offset, side):
    around = lax.rem(info[at.ring] + offset, ring)
    return pl.multiple_of((around * 2 + side) * share, share)


def outer_rows(at, info, k, ring, places, left, full, outs):
    share = outs[0].shape[1]
    picks = [pl.ds(first_row(at, info, ring, share, *place), share) for place in places]
    high, low = (
        jnp.concatenate([part[k, pick, :] for pick in picks], axis=0) for part in left
    )
    product = dot3(high, low, full[0][k], full[1][k])
    target = info[at.target + k]
    for i, out in enumerate(outs):
        out[target] += product[i * share : (i + 1) * share]


def middle_kernel(at, ring, lasts, groups, order, head, info, *refs):
    blocks, refs = refs[: len(lasts)], refs[len(lasts) :]
    parts, refs = refs[: 2 * len(groups)], refs[2 * len(groups) :]
    right_high, right_low, left_high, left_low = refs[:4]
    full_high, full_low = refs[4:6]
    outs, (high, low) = refs[6:-2], refs[-2:]
    share = blocks[0].shape[1]
    side = info[at.side]
    split_blocks(blocks, high, low)
    for out in outs:
        out[...] = jnp.zeros_like(out)
    places = [(r, 1 - side) for r in order[: head[0]]] + [(r, side) for r in order[: head[1]]]

    def put(out, k, r, other, value):
        rows = pl.ds(first_row(at, info, ring, share, r, 1 - side if other else side), share)
        out[k, rows, :] = value

    def one(k, carry):
        source = info[k]
        inner = split(dot3(high[source], low[source], right_high[k], right_low[k]))
        for which, out in enumerate((full_high, full_low)):
            for g, group in enumerate(groups):
                for i, (r, other) in enumerate(group):
                    put(out, k, r, other, parts[2 * g + which][k, i * share : (i + 1) * share, :])
            for i, r in enumerate(lasts):
                put(out, k, r, True, inner[which][i * share : (i + 1) * share])
        outer_rows(
            at, info, k, ring, places, (left_high, left_low), (full_high, full_low), outs
        )
        return carry

    lax.fori_loop(0, info[at.count], one, 0)


def middle(at, info, ring, lasts, groups, order, head, blocks, parts, right, left):
    live, width, _ = right[0].shape
    sectors, share, _ = blocks[0].shape
    count = sum(head)
    results = call(
        functools.partial(middle_kernel, at, ring, lasts, groups, order, head),
        "middle",
        info,
        [*blocks, *(array for part in parts for array in part), *right, *left],
        [((live, width, width), BF16)] * 2 + [(blocks[0].shape, F32)] * count,
        live * share * (len(lasts) + count) * width * width * 6,
        [pltpu.VMEM((sectors, len(lasts) * share, width), BF16)] * 2,
    )
    return results[:2], results[2 : 2 + head[0]], results[2 + head[0] :]


def outer_kernel(at, ring, wanted, counted, info, *refs):
    full_high, full_low, left_high, left_low = refs[:4]
    outs = refs[-len(wanted) :]
    side = info[at.side]
    for out in outs:
        out[...] = jnp.zeros_like(out)
    places = [(r, 1 - side if other else side) for r, other in wanted]

    def one(k, carry):
        outer_rows(
            at, info, k, ring, places, (left_high, left_low), (full_high, full_low), outs
        )
        return carry

    lax.fori_loop(0, info[at.count], one, 0)
    if counted:
        squares, sums = refs[4], refs[-len(wanted) - 1]
        blocks = refs[5 : 5 + 2 * ring]
        totals = [*refs[5 + 2 * ring : 5 + 4 * ring - len(wanted)], *outs]
        dots = sum(lanes(block[...] * total[...]) for block, total in zip(blocks, totals))
        row = lax.broadcasted_iota(jnp.int32, sums.shape, 0)
        sums[...] = jnp.where(row == 0, dots, jnp.where(row == 1, squares[...], 0.0))


def outer_blocks(at, info, ring, wanted, full, left, counted=()):
    live, width, _ = left[0].shape
    share = width // (2 * ring)
    sectors = info.shape[0] - at.limits
    extra = [counted[0], *counted[1], *counted[2]] if counted else []
    return call(
        functools.partial(outer_kernel, at, ring, wanted, bool(counted)),
        "outer_blocks",
        info,
        [*full, *left, *extra],
        ([((8, 128), F32)] if counted else []) + [((sectors, share, width), F32)] * len(wanted),
        0,
    )


def inside(limits, first, start, shape):
    rows = start + lax.broadcasted_iota(jnp.int32, shape[1:], 0)
    cols = lax.broadcasted_iota(jnp.int32, shape[1:], 1)
    return [
        ((rows < limits[first + s]) & (cols < limits[first + s])).astype(F32)
        for s in range(shape[0])
    ]


def begin_kernel(limits, trial, vector, squares):
    total = jnp.zeros(squares.shape, F32)
    start = lax.axis_index("term").astype(jnp.int32) * trial.shape[1]
    for s, mask in enumerate(inside(limits, 0, start, trial.shape)):
        value = mask * trial[s]
        vector[s] = value
        total = total + lanes(value * value)
    squares[...] = total


def begin(limits, trial):
    return call(
        begin_kernel,
        "begin",
        limits,
        [trial],
        [(trial.shape, F32), ((1, 128), F32)],
        trial.size * 4,
    )


def update_kernel(at, ring, info, *refs):
    vector, precond, refs = refs[0], refs[1], refs[2:]
    sums, terms, (result, squares, ritz) = refs[:ring], refs[ring:-3], refs[-3:]
    sums = [part[...] for part in sums]
    while len(sums) > 1:
        half = len(sums) // 2
        sums = [sums[r] + sums[r + half] for r in range(half)]
    both = jnp.sum(sums[0], axis=1, keepdims=True)
    theta = both[0:1] / both[1:2]
    ritz[...] = jnp.broadcast_to(theta, ritz.shape)
    total = jnp.zeros(squares.shape, F32)
    start = (info[at.ring] * 2 + info[at.side]) * vector.shape[1]
    for s, mask in enumerate(inside(info, at.limits, start, vector.shape)):
        sig = mask * sum(term[s] for term in terms)
        value = vector[s] - (sig - theta * vector[s]) / precond[s]
        result[s] = value
        total = total + lanes(value * value)
    squares[...] = total


def update(at, info, vector, precond, sums, terms, ring):
    return call(
        functools.partial(update_kernel, at, ring),
        "update",
        info,
        [vector, precond, *sums, *terms],
        [(vector.shape, F32), ((1, 128), F32), ((1, 128), F32)],
        vector.size * 8,
    )


def across(value, terms):
    return lax.ppermute(value, "term", [(i, i ^ 1) for i in range(terms)])


def around(value, terms, shift):
    return lax.ppermute(value, "term", [(i, (i + 2 * shift) % terms) for i in range(terms)])


def stages(sectors, terms):
    inner = [("term", terms, 1)]
    across_sectors = [("sector", sectors, 1 << bit) for bit in range(sectors.bit_length() - 1)]
    outer = [("term", terms, 1 << bit) for bit in range(1, terms.bit_length() - 1)]
    return inner + across_sectors, outer


def stage_sum(values, stage):
    axis, size, step = stage
    return values + lax.ppermute(values, axis, [(i, i ^ step) for i in range(size)])


def send_order(ring):
    ups = ring // 2
    downs = ring - 1 - ups
    order = []
    for hop in range(ups, 0, -1):
        if hop <= downs:
            order.append((ring - hop) % ring)
        order.append(hop)
    return order + [0]


def scatter_sum(own, other, terms, sums, steps):
    ring = terms // 2
    ups = ring // 2
    downs = ring - 1 - ups
    received = {r: across(other[r], terms) for r in send_order(ring)[:-1]}
    inner, *outer = steps
    block = other[0]
    up = down = None
    for hop in range(ups, 0, -1):
        value = own[hop] + received[hop]
        if up is None:
            value, sums = lax.optimization_barrier((value, sums))
        else:
            value, sums, block = lax.optimization_barrier((value + up, sums, block))
        up = around(value, terms, 1)
        if hop <= downs:
            back = (ring - hop) % ring
            value = own[back] + received[back]
            down = around(value if down is None else value + down, terms, -1)
        if hop == ups:
            sums = stage_sum(sums, inner)
    received[0] = across(block, terms)
    for stage in outer:
        sums = stage_sum(sums, stage)
    parts = [sums] + [around(sums, terms, shift) for shift in range(1, ring)]
    return [term for term in (own[0], received[0], up, down) if term is not None], parts


def per_device(
    trial, precond, sector_dims, left_ops, right_ops, task_source, task_target, task_count
):
    sec_dev, share, width = trial.shape
    slots = left_ops.shape[0]
    sectors, terms = lax.axis_size("sector"), lax.axis_size("term")
    ring = terms // 2
    cells = float(sec_dev * sectors * width * width)
    term = lax.axis_index("term").astype(jnp.int32)
    at = Place(slots)
    info = jnp.concatenate(
        [task_source, task_target, jnp.stack([term // 2, term % 2]), task_count, sector_dims]
    )
    values = []
    vector, squares = begin(sector_dims, trial)
    steps, outer_steps = stages(sectors, terms)
    order = send_order(ring)
    ups = ring // 2
    downs = ring - 1 - ups
    last = ring - ups
    head = (1, 0)
    right, left = split_operators(right_ops, left_ops)
    for step in range(STEPS):
        mine, theirs, groups, parts = {0: vector}, {}, [], []
        token = None
        for hop in range(1, ups + 1):
            value = mine[(ring - hop + 1) % ring]
            if token is not None:
                value, token = lax.optimization_barrier((value, token))
            mine[ring - hop] = around(value, terms, 1)
            fresh = [(ring - hop + 1) % ring]
            if hop <= downs:
                mine[hop] = around(mine[hop - 1], terms, -1)
            if hop > 1 and hop - 1 <= downs:
                fresh.append(hop - 1)
            for r in fresh:
                theirs[r] = across(mine[r], terms)
            if hop == 1:
                group = [(0, False), (0, True)]
            else:
                group = [(r, False) for r in fresh] + before
            before = [(r, True) for r in fresh]
            if hop == 1:
                before = []
            *part, token = inner_rows(
                at,
                info,
                [(theirs if other else mine)[r] for r, other in group],
                right,
                () if token is None else (token,),
            )
            groups.append(group)
            parts.append(part)
        fresh = [last] + ([ups] if ups <= downs else [])
        for r in fresh:
            theirs[r] = across(mine[r], terms)
        lasts = [r for r, _ in before[1:]] + fresh
        group = [(r, False) for r in fresh] + before[:1]
        *part, token = inner_rows(
            at, info, [(theirs if other else mine)[r] for r, other in group], right, (token,)
        )
        groups.append(group)
        parts.append(part)
        full, others, _ = middle(
            at, info, ring, lasts, groups, order, head, [theirs[r] for r in lasts], parts, right, left
        )
        done = [(r, True) for r in order[:1]]
        totals = dict(zip(done, others))
        first = [(r, True) for r in order[1:-1]] + [(r, False) for r in order[:2]]
        totals.update(zip(first, outer_blocks(at, info, ring, first, full, left)))
        done += first
        rest = [(r, True) for r in order[-1:]] + [(r, False) for r in order[2:]]
        blocks = [(theirs if other else mine)[r] for r, other in done + rest]
        sums, *outs = outer_blocks(
            at, info, ring, rest, full, left, (squares, blocks, [totals[key] for key in done])
        )
        totals.update(zip(rest, outs))
        owns = {r: totals[r, False] for r in range(ring)}
        others = {r: totals[r, True] for r in range(ring)}
        summed, sums = scatter_sum(owns, others, terms, sums, steps)
        vector, squares, ritz = update(at, info, vector, precond, sums, summed, ring)
        values.append(ritz[0, :1])
    for stage in steps + outer_steps:
        squares = stage_sum(squares, stage)
    return (vector * jnp.sqrt(cells / jnp.sum(squares)), jnp.concatenate(values))


def solution(mesh):
    return jax.shard_map(
        per_device,
        mesh=mesh,
        in_specs=(
            P("sector", "term", None),
            P("sector", "term", None),
            P("sector"),
            P(("sector", "term"), None, None),
            P(("sector", "term"), None, None),
            P(("sector", "term")),
            P(("sector", "term")),
            P(("sector", "term")),
        ),
        out_specs=(P("sector", "term", None), P()),
        check_vma=False,
    )
```

```python
import functools

import jax
import jax.numpy as jnp
from jax import lax
from jax.experimental import pallas as pl
from jax.experimental.pallas import tpu as pltpu
from jax.sharding import PartitionSpec as P

STEPS = 3
VMEM_LIMIT = 4 * 1024 * 1024
SPLIT_VMEM_LIMIT = 9 * 1024 * 1024
F32 = jnp.float32
BF16 = jnp.bfloat16


def split(value):
    high = value.astype(BF16)
    return high, (value - high.astype(F32)).astype(BF16)


def dot3(a_high, a_low, b_high, b_low):
    def dot(a, b):
        return jnp.dot(a, b, preferred_element_type=F32)

    rows = a_high.shape[0]
    both = dot(jnp.concatenate([a_high, a_low], axis=0), b_high)
    return both[:rows] + (both[rows:] + dot(a_high, b_low))


def call(kernel, name, info, arrays, results, flops, scratch=()):
    held = pl.BlockSpec(memory_space=pltpu.VMEM)
    return pl.pallas_call(
        kernel,
        in_specs=[pl.BlockSpec(memory_space=pltpu.SMEM)] + [held] * len(arrays),
        out_specs=[held] * len(results),
        out_shape=[pltpu.VMEM(shape, dtype) for shape, dtype in results],
        scratch_shapes=list(scratch),
        compiler_params=pltpu.CompilerParams(vmem_limit_bytes=VMEM_LIMIT),
        cost_estimate=pl.CostEstimate(flops=flops, bytes_accessed=0, transcendentals=0),
        name=name,
    )(info, *arrays)


class Place:
    def __init__(self, slots):
        self.target, self.ring, self.side = slots, 2 * slots, 2 * slots + 1
        self.count, self.limits = 2 * slots + 2, 2 * slots + 3


def split_kernel(operators, *refs):
    high, low, held, ready = refs[-4:]
    live = held.shape[0]

    def copy(k):
        return pltpu.make_async_copy(operators.at[k], held.at[k], ready.at[k])

    for k in range(live):
        copy(k).start()

    def one(k, carry):
        copy(k).wait()
        high[k], low[k] = split(held[k])
        return carry

    lax.fori_loop(0, live, one, 0)


def split_operators(operators, name, earlier=()):
    slots, width, _ = operators.shape
    shape = (slots - 1, width, width)
    return pl.pallas_call(
        split_kernel,
        in_specs=[pl.BlockSpec(memory_space=pltpu.HBM)]
        + [pl.BlockSpec(memory_space=pltpu.VMEM)] * len(earlier),
        out_specs=[pl.BlockSpec(memory_space=pltpu.VMEM)] * 2,
        out_shape=[pltpu.VMEM(shape, BF16)] * 2,
        scratch_shapes=[pltpu.VMEM(shape, F32), pltpu.SemaphoreType.DMA((slots - 1,))],
        compiler_params=pltpu.CompilerParams(vmem_limit_bytes=SPLIT_VMEM_LIMIT),
        cost_estimate=pl.CostEstimate(flops=0, bytes_accessed=operators.size * 4, transcendentals=0),
        name=name,
    )(pltpu.with_memory_space_constraint(operators, pltpu.HBM), *earlier)


def split_blocks(blocks, high, low):
    share = blocks[0].shape[1]
    for place, block in enumerate(blocks):
        rows = pl.ds(place * share, share)
        high[:, rows, :], low[:, rows, :] = split(block[...])


def lanes(value):
    total = jnp.sum(value, axis=tuple(range(value.ndim - 1)))[None]
    width = total.shape[1]
    return sum(total[:, c : c + 128] for c in range(0, width, 128))


def inner_kernel(at, ring, info, *refs):
    blocks = refs[:ring]
    right_high, right_low = refs[ring : ring + 2]
    out_high, out_low, token, high, low = refs[-5:]
    token[...] = jnp.zeros_like(token)
    split_blocks(blocks, high, low)

    def one(k, carry):
        source = info[k]
        out_high[k], out_low[k] = split(
            dot3(high[source], low[source], right_high[k], right_low[k])
        )
        return carry

    lax.fori_loop(0, info[at.count], one, 0)


def inner_rows(at, info, blocks, right, earlier=()):
    ring = len(blocks)
    live, width, _ = right[0].shape
    sectors, share, _ = blocks[0].shape
    rows = ring * share
    return call(
        functools.partial(inner_kernel, at, ring),
        "inner_rows",
        info,
        [*blocks, *right, *earlier],
        [((live, rows, width), BF16)] * 2 + [((1, 128), F32)],
        live * rows * width * width * 6,
        [pltpu.VMEM((sectors, rows, width), BF16)] * 2,
    )


def first_row(at, info, ring, share, offset, side):
    around = lax.rem(info[at.ring] + offset, ring)
    return pl.multiple_of((around * 2 + side) * share, share)


def outer_rows(at, info, k, ring, places, left, full, outs):
    share = outs[0].shape[1]
    picks = [pl.ds(first_row(at, info, ring, share, *place), share) for place in places]
    high, low = (
        jnp.concatenate([part[k, pick, :] for pick in picks], axis=0) for part in left
    )
    product = dot3(high, low, full[0][k], full[1][k])
    target = info[at.target + k]
    for i, out in enumerate(outs):
        out[target] += product[i * share : (i + 1) * share]


def middle_kernel(at, ring, lasts, groups, order, head, info, *refs):
    blocks, refs = refs[: len(lasts)], refs[len(lasts) :]
    parts, refs = refs[: 2 * len(groups)], refs[2 * len(groups) :]
    right_high, right_low, left_high, left_low = refs[:4]
    full_high, full_low = refs[4:6]
    outs, (high, low) = refs[6:-2], refs[-2:]
    share = blocks[0].shape[1]
    side = info[at.side]
    split_blocks(blocks, high, low)
    for out in outs:
        out[...] = jnp.zeros_like(out)
    places = [(r, 1 - side) for r in order[: head[0]]] + [(r, side) for r in order[: head[1]]]

    def put(out, k, r, other, value):
        rows = pl.ds(first_row(at, info, ring, share, r, 1 - side if other else side), share)
        out[k, rows, :] = value

    def one(k, carry):
        source = info[k]
        inner = split(dot3(high[source], low[source], right_high[k], right_low[k]))
        for which, out in enumerate((full_high, full_low)):
            for g, group in enumerate(groups):
                for i, (r, other) in enumerate(group):
                    put(out, k, r, other, parts[2 * g + which][k, i * share : (i + 1) * share, :])
            for i, r in enumerate(lasts):
                put(out, k, r, True, inner[which][i * share : (i + 1) * share])
        outer_rows(
            at, info, k, ring, places, (left_high, left_low), (full_high, full_low), outs
        )
        return carry

    lax.fori_loop(0, info[at.count], one, 0)


def middle(at, info, ring, lasts, groups, order, head, blocks, parts, right, left):
    live, width, _ = right[0].shape
    sectors, share, _ = blocks[0].shape
    count = sum(head)
    results = call(
        functools.partial(middle_kernel, at, ring, lasts, groups, order, head),
        "middle",
        info,
        [*blocks, *(array for part in parts for array in part), *right, *left],
        [((live, width, width), BF16)] * 2 + [(blocks[0].shape, F32)] * count,
        live * share * (len(lasts) + count) * width * width * 6,
        [pltpu.VMEM((sectors, len(lasts) * share, width), BF16)] * 2,
    )
    return results[:2], results[2 : 2 + head[0]], results[2 + head[0] :]


def outer_kernel(at, ring, wanted, counted, info, *refs):
    full_high, full_low, left_high, left_low = refs[:4]
    outs = refs[-len(wanted) :]
    side = info[at.side]
    for out in outs:
        out[...] = jnp.zeros_like(out)
    places = [(r, 1 - side if other else side) for r, other in wanted]

    def one(k, carry):
        outer_rows(
            at, info, k, ring, places, (left_high, left_low), (full_high, full_low), outs
        )
        return carry

    lax.fori_loop(0, info[at.count], one, 0)
    if counted:
        squares, sums = refs[4], refs[-len(wanted) - 1]
        blocks = refs[5 : 5 + 2 * ring]
        totals = [*refs[5 + 2 * ring : 5 + 4 * ring - len(wanted)], *outs]
        dots = sum(lanes(block[...] * total[...]) for block, total in zip(blocks, totals))
        row = lax.broadcasted_iota(jnp.int32, sums.shape, 0)
        sums[...] = jnp.where(row == 0, dots, jnp.where(row == 1, squares[...], 0.0))


def outer_blocks(at, info, ring, wanted, full, left, counted=()):
    live, width, _ = left[0].shape
    share = width // (2 * ring)
    sectors = info.shape[0] - at.limits
    extra = [counted[0], *counted[1], *counted[2]] if counted else []
    return call(
        functools.partial(outer_kernel, at, ring, wanted, bool(counted)),
        "outer_blocks",
        info,
        [*full, *left, *extra],
        ([((8, 128), F32)] if counted else []) + [((sectors, share, width), F32)] * len(wanted),
        0,
    )


def inside(limits, first, start, shape):
    rows = start + lax.broadcasted_iota(jnp.int32, shape[1:], 0)
    cols = lax.broadcasted_iota(jnp.int32, shape[1:], 1)
    return [
        ((rows < limits[first + s]) & (cols < limits[first + s])).astype(F32)
        for s in range(shape[0])
    ]


def begin_kernel(limits, trial, vector, squares):
    total = jnp.zeros(squares.shape, F32)
    start = lax.axis_index("term").astype(jnp.int32) * trial.shape[1]
    for s, mask in enumerate(inside(limits, 0, start, trial.shape)):
        value = mask * trial[s]
        vector[s] = value
        total = total + lanes(value * value)
    squares[...] = total


def begin(limits, trial):
    return call(
        begin_kernel,
        "begin",
        limits,
        [trial],
        [(trial.shape, F32), ((1, 128), F32)],
        trial.size * 4,
    )


def update_kernel(at, ring, info, *refs):
    vector, precond, refs = refs[0], refs[1], refs[2:]
    sums, terms, (result, squares, ritz) = refs[:ring], refs[ring:-3], refs[-3:]
    sums = [part[...] for part in sums]
    while len(sums) > 1:
        half = len(sums) // 2
        sums = [sums[r] + sums[r + half] for r in range(half)]
    both = jnp.sum(sums[0], axis=1, keepdims=True)
    theta = both[0:1] / both[1:2]
    ritz[...] = jnp.broadcast_to(theta, ritz.shape)
    total = jnp.zeros(squares.shape, F32)
    start = (info[at.ring] * 2 + info[at.side]) * vector.shape[1]
    for s, mask in enumerate(inside(info, at.limits, start, vector.shape)):
        sig = mask * sum(term[s] for term in terms)
        value = vector[s] - (sig - theta * vector[s]) / precond[s]
        result[s] = value
        total = total + lanes(value * value)
    squares[...] = total


def update(at, info, vector, precond, sums, terms, ring):
    return call(
        functools.partial(update_kernel, at, ring),
        "update",
        info,
        [vector, precond, *sums, *terms],
        [(vector.shape, F32), ((1, 128), F32), ((1, 128), F32)],
        vector.size * 8,
    )


def across(value, terms):
    return lax.ppermute(value, "term", [(i, i ^ 1) for i in range(terms)])


def around(value, terms, shift):
    return lax.ppermute(value, "term", [(i, (i + 2 * shift) % terms) for i in range(terms)])


def stages(sectors, terms):
    inner = [("term", terms, 1)]
    across_sectors = [("sector", sectors, 1 << bit) for bit in range(sectors.bit_length() - 1)]
    outer = [("term", terms, 1 << bit) for bit in range(1, terms.bit_length() - 1)]
    return inner + across_sectors, outer


def stage_sum(values, stage):
    axis, size, step = stage
    return values + lax.ppermute(values, axis, [(i, i ^ step) for i in range(size)])


def send_order(ring):
    ups = ring // 2
    downs = ring - 1 - ups
    order = []
    for hop in range(ups, 0, -1):
        order.append(hop)
        if hop <= downs:
            order.append((ring - hop) % ring)
    return order + [0]


def scatter_sum(own, other, terms, sums, steps):
    ring = terms // 2
    ups = ring // 2
    downs = ring - 1 - ups
    received = {r: across(other[r], terms) for r in send_order(ring)}
    inner, *outer = steps
    sums = stage_sum(sums, inner)
    up = down = None
    for hop in range(ups, 0, -1):
        value = own[hop] + received[hop]
        value, sums = lax.optimization_barrier((value if up is None else value + up, sums))
        up = around(value, terms, 1)
        if hop == ups:
            for stage in outer:
                sums = stage_sum(sums, stage)
        if hop <= downs:
            back = (ring - hop) % ring
            value = own[back] + received[back]
            value, sums = lax.optimization_barrier((value if down is None else value + down, sums))
            down = around(value, terms, -1)
    parts = [sums] + [around(sums, terms, shift) for shift in range(1, ring)]
    return [term for term in (own[0], received[0], up, down) if term is not None], parts


def per_device(
    trial, precond, sector_dims, left_ops, right_ops, task_source, task_target, task_count
):
    sec_dev, share, width = trial.shape
    slots = left_ops.shape[0]
    sectors, terms = lax.axis_size("sector"), lax.axis_size("term")
    ring = terms // 2
    cells = float(sec_dev * sectors * width * width)
    term = lax.axis_index("term").astype(jnp.int32)
    at = Place(slots)
    info = jnp.concatenate(
        [task_source, task_target, jnp.stack([term // 2, term % 2]), task_count, sector_dims]
    )
    values = []
    vector, squares = begin(sector_dims, trial)
    steps, outer_steps = stages(sectors, terms)
    order = send_order(ring)
    ups = ring // 2
    downs = ring - 1 - ups
    last = ring - ups
    head = (ring // 2, ring // 4)
    right = left = None
    for step in range(STEPS):
        mine, theirs, groups, parts = {0: vector}, {}, [], []
        token = None
        for hop in range(1, ups + 1):
            value = mine[(ring - hop + 1) % ring]
            if token is not None:
                value, token = lax.optimization_barrier((value, token))
            mine[ring - hop] = around(value, terms, 1)
            fresh = [(ring - hop + 1) % ring]
            if hop <= downs:
                mine[hop] = around(mine[hop - 1], terms, -1)
            if hop > 1 and hop - 1 <= downs:
                fresh.append(hop - 1)
            for r in fresh:
                theirs[r] = across(mine[r], terms)
            if hop == 1:
                group = [(0, False), (0, True)]
            else:
                group = [(r, False) for r in fresh] + before
            before = [(r, True) for r in fresh]
            if hop == 1:
                before = []
            if right is None:
                right = split_operators(right_ops, "split_right", (theirs[0],))
            *part, token = inner_rows(
                at,
                info,
                [(theirs if other else mine)[r] for r, other in group],
                right,
                () if token is None else (token,),
            )
            groups.append(group)
            parts.append(part)
            if left is None:
                left = split_operators(left_ops, "split_left", (token, mine[1]))
        fresh = [last] + ([ups] if ups <= downs else [])
        for r in fresh:
            theirs[r] = across(mine[r], terms)
        lasts = [r for r, _ in before[1:]] + fresh
        group = [(r, False) for r in fresh] + before[:1]
        *part, token = inner_rows(
            at, info, [(theirs if other else mine)[r] for r, other in group], right, (token,)
        )
        groups.append(group)
        parts.append(part)
        full, others, owns = middle(
            at, info, ring, lasts, groups, order, head, [theirs[r] for r in lasts], parts, right, left
        )
        done = [(r, True) for r in order[: head[0]]] + [(r, False) for r in order[: head[1]]]
        totals = dict(zip(done, [*others, *owns]))
        rest = [(r, True) for r in order[head[0] :]] + [(r, False) for r in order[head[1] :]]
        blocks = [(theirs if other else mine)[r] for r, other in done + rest]
        sums, *outs = outer_blocks(
            at, info, ring, rest, full, left, (squares, blocks, [totals[key] for key in done])
        )
        totals.update(zip(rest, outs))
        owns = {r: totals[r, False] for r in range(ring)}
        others = {r: totals[r, True] for r in range(ring)}
        summed, sums = scatter_sum(owns, others, terms, sums, steps)
        vector, squares, ritz = update(at, info, vector, precond, sums, summed, ring)
        values.append(ritz[0, :1])
    for stage in steps + outer_steps:
        squares = stage_sum(squares, stage)
    return (vector * jnp.sqrt(cells / jnp.sum(squares)), jnp.concatenate(values))


def solution(mesh):
    return jax.shard_map(
        per_device,
        mesh=mesh,
        in_specs=(
            P("sector", "term", None),
            P("sector", "term", None),
            P("sector"),
            P(("sector", "term"), None, None),
            P(("sector", "term"), None, None),
            P(("sector", "term")),
            P(("sector", "term")),
            P(("sector", "term")),
        ),
        out_specs=(P("sector", "term", None), P()),
        check_vma=False,
    )
```

```python
import functools

import jax
import jax.numpy as jnp
from jax import lax
from jax.experimental import pallas as pl
from jax.experimental.pallas import tpu as pltpu
from jax.sharding import PartitionSpec as P

STEPS = 3
VMEM_LIMIT = 4 * 1024 * 1024
SPLIT_VMEM_LIMIT = 9 * 1024 * 1024
F32 = jnp.float32
BF16 = jnp.bfloat16


def split(value):
    high = value.astype(BF16)
    return high, (value - high.astype(F32)).astype(BF16)


def dot3(a_high, a_low, b_high, b_low):
    def dot(a, b):
        return jnp.dot(a, b, preferred_element_type=F32)

    rows = a_high.shape[0]
    both = dot(jnp.concatenate([a_high, a_low], axis=0), b_high)
    return both[:rows] + (both[rows:] + dot(a_high, b_low))


def call(kernel, name, info, arrays, results, flops, scratch=()):
    held = pl.BlockSpec(memory_space=pltpu.VMEM)
    return pl.pallas_call(
        kernel,
        in_specs=[pl.BlockSpec(memory_space=pltpu.SMEM)] + [held] * len(arrays),
        out_specs=[held] * len(results),
        out_shape=[pltpu.VMEM(shape, dtype) for shape, dtype in results],
        scratch_shapes=list(scratch),
        compiler_params=pltpu.CompilerParams(vmem_limit_bytes=VMEM_LIMIT),
        cost_estimate=pl.CostEstimate(flops=flops, bytes_accessed=0, transcendentals=0),
        name=name,
    )(info, *arrays)


class Place:
    def __init__(self, slots):
        self.target, self.ring, self.side = slots, 2 * slots, 2 * slots + 1
        self.count, self.limits = 2 * slots + 2, 2 * slots + 3


def split_kernel(operators, *refs):
    high, low, held, ready = refs[-4:]
    live = held.shape[0]

    def copy(k):
        return pltpu.make_async_copy(operators.at[k], held.at[k], ready.at[k])

    for k in range(live):
        copy(k).start()

    def one(k, carry):
        copy(k).wait()
        high[k], low[k] = split(held[k])
        return carry

    lax.fori_loop(0, live, one, 0)


def split_operators(operators, name, earlier=()):
    slots, width, _ = operators.shape
    shape = (slots - 1, width, width)
    return pl.pallas_call(
        split_kernel,
        in_specs=[pl.BlockSpec(memory_space=pltpu.HBM)]
        + [pl.BlockSpec(memory_space=pltpu.VMEM)] * len(earlier),
        out_specs=[pl.BlockSpec(memory_space=pltpu.VMEM)] * 2,
        out_shape=[pltpu.VMEM(shape, BF16)] * 2,
        scratch_shapes=[pltpu.VMEM(shape, F32), pltpu.SemaphoreType.DMA((slots - 1,))],
        compiler_params=pltpu.CompilerParams(vmem_limit_bytes=SPLIT_VMEM_LIMIT),
        cost_estimate=pl.CostEstimate(flops=0, bytes_accessed=operators.size * 4, transcendentals=0),
        name=name,
    )(pltpu.with_memory_space_constraint(operators, pltpu.HBM), *earlier)


def split_blocks(blocks, high, low):
    share = blocks[0].shape[1]
    for place, block in enumerate(blocks):
        rows = pl.ds(place * share, share)
        high[:, rows, :], low[:, rows, :] = split(block[...])


def lanes(value):
    total = jnp.sum(value, axis=tuple(range(value.ndim - 1)))[None]
    width = total.shape[1]
    return sum(total[:, c : c + 128] for c in range(0, width, 128))


def each_live(count, one):
    def pair(i, carry):
        one(2 * i, carry)
        return one(2 * i + 1, carry)

    pairs = lax.div(count, 2)
    lax.fori_loop(0, pairs, pair, 0)
    lax.fori_loop(2 * pairs, count, one, 0)


def inner_kernel(at, ring, info, *refs):
    blocks = refs[:ring]
    right_high, right_low = refs[ring : ring + 2]
    out_high, out_low, token, high, low = refs[-5:]
    token[...] = jnp.zeros_like(token)
    split_blocks(blocks, high, low)

    def one(k, carry):
        source = info[k]
        out_high[k], out_low[k] = split(
            dot3(high[source], low[source], right_high[k], right_low[k])
        )
        return carry

    each_live(info[at.count], one)


def inner_rows(at, info, blocks, right, earlier=()):
    ring = len(blocks)
    live, width, _ = right[0].shape
    sectors, share, _ = blocks[0].shape
    rows = ring * share
    return call(
        functools.partial(inner_kernel, at, ring),
        "inner_rows",
        info,
        [*blocks, *right, *earlier],
        [((live, rows, width), BF16)] * 2 + [((1, 128), F32)],
        live * rows * width * width * 6,
        [pltpu.VMEM((sectors, rows, width), BF16)] * 2,
    )


def first_row(at, info, ring, share, offset, side):
    around = lax.rem(info[at.ring] + offset, ring)
    return pl.multiple_of((around * 2 + side) * share, share)


def outer_rows(at, info, k, ring, places, left, full, outs):
    share = outs[0].shape[1]
    picks = [pl.ds(first_row(at, info, ring, share, *place), share) for place in places]
    high, low = (
        jnp.concatenate([part[k, pick, :] for pick in picks], axis=0) for part in left
    )
    product = dot3(high, low, full[0][k], full[1][k])
    target = info[at.target + k]
    for i, out in enumerate(outs):
        out[target] += product[i * share : (i + 1) * share]


def middle_kernel(at, ring, lasts, groups, order, head, info, *refs):
    blocks, refs = refs[: len(lasts)], refs[len(lasts) :]
    parts, refs = refs[: 2 * len(groups)], refs[2 * len(groups) :]
    right_high, right_low, left_high, left_low = refs[:4]
    full_high, full_low = refs[4:6]
    outs, (high, low) = refs[6:-2], refs[-2:]
    share = blocks[0].shape[1]
    side = info[at.side]
    split_blocks(blocks, high, low)
    for out in outs:
        out[...] = jnp.zeros_like(out)
    places = [(r, 1 - side) for r in order[: head[0]]] + [(r, side) for r in order[: head[1]]]

    def put(out, k, r, other, value):
        rows = pl.ds(first_row(at, info, ring, share, r, 1 - side if other else side), share)
        out[k, rows, :] = value

    def one(k, carry):
        source = info[k]
        inner = split(dot3(high[source], low[source], right_high[k], right_low[k]))
        for which, out in enumerate((full_high, full_low)):
            for g, group in enumerate(groups):
                for i, (r, other) in enumerate(group):
                    put(out, k, r, other, parts[2 * g + which][k, i * share : (i + 1) * share, :])
            for i, r in enumerate(lasts):
                put(out, k, r, True, inner[which][i * share : (i + 1) * share])
        outer_rows(
            at, info, k, ring, places, (left_high, left_low), (full_high, full_low), outs
        )
        return carry

    each_live(info[at.count], one)


def middle(at, info, ring, lasts, groups, order, head, blocks, parts, right, left):
    live, width, _ = right[0].shape
    sectors, share, _ = blocks[0].shape
    count = sum(head)
    results = call(
        functools.partial(middle_kernel, at, ring, lasts, groups, order, head),
        "middle",
        info,
        [*blocks, *(array for part in parts for array in part), *right, *left],
        [((live, width, width), BF16)] * 2 + [(blocks[0].shape, F32)] * count,
        live * share * (len(lasts) + count) * width * width * 6,
        [pltpu.VMEM((sectors, len(lasts) * share, width), BF16)] * 2,
    )
    return results[:2], results[2 : 2 + head[0]], results[2 + head[0] :]


def outer_kernel(at, ring, wanted, counted, info, *refs):
    full_high, full_low, left_high, left_low = refs[:4]
    outs = refs[-len(wanted) :]
    side = info[at.side]
    for out in outs:
        out[...] = jnp.zeros_like(out)
    places = [(r, 1 - side if other else side) for r, other in wanted]

    def one(k, carry):
        outer_rows(
            at, info, k, ring, places, (left_high, left_low), (full_high, full_low), outs
        )
        return carry

    each_live(info[at.count], one)
    if counted:
        squares, sums = refs[4], refs[-len(wanted) - 1]
        blocks = refs[5 : 5 + 2 * ring]
        totals = [*refs[5 + 2 * ring : 5 + 4 * ring - len(wanted)], *outs]
        dots = sum(lanes(block[...] * total[...]) for block, total in zip(blocks, totals))
        row = lax.broadcasted_iota(jnp.int32, sums.shape, 0)
        sums[...] = jnp.where(row == 0, dots, jnp.where(row == 1, squares[...], 0.0))


def outer_blocks(at, info, ring, wanted, full, left, counted=()):
    live, width, _ = left[0].shape
    share = width // (2 * ring)
    sectors = info.shape[0] - at.limits
    extra = [counted[0], *counted[1], *counted[2]] if counted else []
    return call(
        functools.partial(outer_kernel, at, ring, wanted, bool(counted)),
        "outer_blocks",
        info,
        [*full, *left, *extra],
        ([((8, 128), F32)] if counted else []) + [((sectors, share, width), F32)] * len(wanted),
        0,
    )


def inside(limits, first, start, shape):
    rows = start + lax.broadcasted_iota(jnp.int32, shape[1:], 0)
    cols = lax.broadcasted_iota(jnp.int32, shape[1:], 1)
    return [
        ((rows < limits[first + s]) & (cols < limits[first + s])).astype(F32)
        for s in range(shape[0])
    ]


def begin_kernel(limits, trial, vector, squares):
    total = jnp.zeros(squares.shape, F32)
    start = lax.axis_index("term").astype(jnp.int32) * trial.shape[1]
    for s, mask in enumerate(inside(limits, 0, start, trial.shape)):
        value = mask * trial[s]
        vector[s] = value
        total = total + lanes(value * value)
    squares[...] = total


def begin(limits, trial):
    return call(
        begin_kernel,
        "begin",
        limits,
        [trial],
        [(trial.shape, F32), ((1, 128), F32)],
        trial.size * 4,
    )


def ring_sum(parts):
    parts = [part[...] for part in parts]
    while len(parts) > 1:
        half = len(parts) // 2
        parts = [parts[r] + parts[r + half] for r in range(half)]
    return parts[0]


def finish_kernel(cells, vector, *refs):
    parts, result = refs[:-1], refs[-1]
    total = jnp.sum(ring_sum(parts), axis=1, keepdims=True)
    scale = jnp.sqrt(cells / total)
    for s in range(vector.shape[0]):
        result[s] = vector[s] * scale


def finish(cells, vector, parts):
    return pl.pallas_call(
        functools.partial(finish_kernel, cells),
        in_specs=[pl.BlockSpec(memory_space=pltpu.VMEM)] * (1 + len(parts)),
        out_specs=pl.BlockSpec(memory_space=pltpu.VMEM),
        out_shape=jax.ShapeDtypeStruct(vector.shape, F32),
        compiler_params=pltpu.CompilerParams(vmem_limit_bytes=VMEM_LIMIT),
        name="finish",
    )(vector, *parts)


def update_kernel(at, ring, info, *refs):
    vector, precond, refs = refs[0], refs[1], refs[2:]
    sums, terms, (result, squares, ritz) = refs[:ring], refs[ring:-3], refs[-3:]
    both = jnp.sum(ring_sum(sums), axis=1, keepdims=True)
    theta = both[0:1] / both[1:2]
    ritz[...] = jnp.broadcast_to(theta, ritz.shape)
    total = jnp.zeros(squares.shape, F32)
    start = (info[at.ring] * 2 + info[at.side]) * vector.shape[1]
    for s, mask in enumerate(inside(info, at.limits, start, vector.shape)):
        sig = mask * sum(term[s] for term in terms)
        value = vector[s] - (sig - theta * vector[s]) / precond[s]
        result[s] = value
        total = total + lanes(value * value)
    squares[...] = total


def update(at, info, vector, precond, sums, terms, ring):
    return call(
        functools.partial(update_kernel, at, ring),
        "update",
        info,
        [vector, precond, *sums, *terms],
        [(vector.shape, F32), ((1, 128), F32), ((1, 128), F32)],
        vector.size * 8,
    )


def across(value, terms):
    return lax.ppermute(value, "term", [(i, i ^ 1) for i in range(terms)])


def around(value, terms, shift):
    return lax.ppermute(value, "term", [(i, (i + 2 * shift) % terms) for i in range(terms)])


def stages(sectors, terms):
    inner = [("term", terms, 1)]
    across_sectors = [("sector", sectors, 1 << bit) for bit in range(sectors.bit_length() - 1)]
    outer = [("term", terms, 1 << bit) for bit in range(1, terms.bit_length() - 1)]
    return inner + across_sectors, outer


def stage_sum(values, stage):
    axis, size, step = stage
    return values + lax.ppermute(values, axis, [(i, i ^ step) for i in range(size)])


def send_order(ring):
    ups = ring // 2
    downs = ring - 1 - ups
    order = []
    for hop in range(ups, 0, -1):
        order.append(hop)
        if hop <= downs:
            order.append((ring - hop) % ring)
    return order + [0]


def scatter_sum(own, other, terms, sums, steps):
    ring = terms // 2
    ups = ring // 2
    downs = ring - 1 - ups
    received = {r: across(other[r], terms) for r in send_order(ring)}
    inner, *outer = steps
    sums = stage_sum(sums, inner)
    up = down = None
    for hop in range(ups, 0, -1):
        value = own[hop] + received[hop]
        value, sums = lax.optimization_barrier((value if up is None else value + up, sums))
        up = around(value, terms, 1)
        if hop == ups:
            for stage in outer:
                sums = stage_sum(sums, stage)
        if hop <= downs:
            back = (ring - hop) % ring
            value = own[back] + received[back]
            value, sums = lax.optimization_barrier((value if down is None else value + down, sums))
            down = around(value, terms, -1)
    parts = [sums] + [around(sums, terms, shift) for shift in range(1, ring)]
    return [term for term in (own[0], received[0], up, down) if term is not None], parts


def per_device(
    trial, precond, sector_dims, left_ops, right_ops, task_source, task_target, task_count
):
    sec_dev, share, width = trial.shape
    slots = left_ops.shape[0]
    sectors, terms = lax.axis_size("sector"), lax.axis_size("term")
    ring = terms // 2
    cells = float(sec_dev * sectors * width * width)
    term = lax.axis_index("term").astype(jnp.int32)
    at = Place(slots)
    info = jnp.concatenate(
        [task_source, task_target, jnp.stack([term // 2, term % 2]), task_count, sector_dims]
    )
    values = []
    vector, squares = begin(sector_dims, trial)
    steps, outer_steps = stages(sectors, terms)
    order = send_order(ring)
    ups = ring // 2
    downs = ring - 1 - ups
    last = ring - ups
    head = (ring // 2, ring // 4)
    right = left = None
    for step in range(STEPS):
        mine, theirs, groups, parts = {0: vector}, {}, [], []
        token = None
        for hop in range(1, ups + 1):
            value = mine[(ring - hop + 1) % ring]
            if token is not None:
                value, token = lax.optimization_barrier((value, token))
            mine[ring - hop] = around(value, terms, 1)
            fresh = [(ring - hop + 1) % ring]
            if hop <= downs:
                mine[hop] = around(mine[hop - 1], terms, -1)
            if hop > 1 and hop - 1 <= downs:
                fresh.append(hop - 1)
            for r in fresh:
                theirs[r] = across(mine[r], terms)
            if hop == 1:
                group = [(0, False), (0, True)]
            else:
                group = [(r, False) for r in fresh] + before
            before = [(r, True) for r in fresh]
            if hop == 1:
                before = []
            if right is None:
                right = split_operators(right_ops, "split_right", (theirs[0],))
            *part, token = inner_rows(
                at,
                info,
                [(theirs if other else mine)[r] for r, other in group],
                right,
                () if token is None else (token,),
            )
            groups.append(group)
            parts.append(part)
            if left is None:
                left = split_operators(left_ops, "split_left", (token, mine[1]))
        fresh = [last] + ([ups] if ups <= downs else [])
        for r in fresh:
            theirs[r] = across(mine[r], terms)
        lasts = [r for r, _ in before[1:]] + fresh
        group = [(r, False) for r in fresh] + before[:1]
        *part, token = inner_rows(
            at, info, [(theirs if other else mine)[r] for r, other in group], right, (token,)
        )
        groups.append(group)
        parts.append(part)
        full, others, owns = middle(
            at, info, ring, lasts, groups, order, head, [theirs[r] for r in lasts], parts, right, left
        )
        done = [(r, True) for r in order[: head[0]]] + [(r, False) for r in order[: head[1]]]
        totals = dict(zip(done, [*others, *owns]))
        rest = [(r, True) for r in order[head[0] :]] + [(r, False) for r in order[head[1] :]]
        blocks = [(theirs if other else mine)[r] for r, other in done + rest]
        sums, *outs = outer_blocks(
            at, info, ring, rest, full, left, (squares, blocks, [totals[key] for key in done])
        )
        totals.update(zip(rest, outs))
        owns = {r: totals[r, False] for r in range(ring)}
        others = {r: totals[r, True] for r in range(ring)}
        summed, sums = scatter_sum(owns, others, terms, sums, steps)
        vector, squares, ritz = update(at, info, vector, precond, sums, summed, ring)
        values.append(ritz[0, :1])
    for stage in steps + outer_steps:
        squares = stage_sum(squares, stage)
    return (finish(cells, vector, [squares]), jnp.concatenate(values))


def solution(mesh):
    return jax.shard_map(
        per_device,
        mesh=mesh,
        in_specs=(
            P("sector", "term", None),
            P("sector", "term", None),
            P("sector"),
            P(("sector", "term"), None, None),
            P(("sector", "term"), None, None),
            P(("sector", "term")),
            P(("sector", "term")),
            P(("sector", "term")),
        ),
        out_specs=(P("sector", "term", None), P()),
        check_vma=False,
    )
```

```python
import functools

import jax
import jax.numpy as jnp
from jax import lax
from jax.experimental import pallas as pl
from jax.experimental.pallas import tpu as pltpu
from jax.sharding import PartitionSpec as P

STEPS = 3
VMEM_LIMIT = 4 * 1024 * 1024
SPLIT_VMEM_LIMIT = 9 * 1024 * 1024
F32 = jnp.float32
BF16 = jnp.bfloat16


def split(value):
    high = value.astype(BF16)
    return high, (value - high.astype(F32)).astype(BF16)


def dot3(a_high, a_low, b_high, b_low):
    def dot(a, b):
        return jnp.dot(a, b, preferred_element_type=F32)

    rows = a_high.shape[0]
    both = dot(jnp.concatenate([a_high, a_low], axis=0), b_high)
    return both[:rows] + (both[rows:] + dot(a_high, b_low))


def call(kernel, name, info, arrays, results, flops, scratch=()):
    held = pl.BlockSpec(memory_space=pltpu.VMEM)
    return pl.pallas_call(
        kernel,
        in_specs=[pl.BlockSpec(memory_space=pltpu.SMEM)] + [held] * len(arrays),
        out_specs=[held] * len(results),
        out_shape=[pltpu.VMEM(shape, dtype) for shape, dtype in results],
        scratch_shapes=list(scratch),
        compiler_params=pltpu.CompilerParams(vmem_limit_bytes=VMEM_LIMIT),
        cost_estimate=pl.CostEstimate(flops=flops, bytes_accessed=0, transcendentals=0),
        name=name,
    )(info, *arrays)


class Place:
    def __init__(self, slots):
        self.target, self.ring, self.side = slots, 2 * slots, 2 * slots + 1
        self.count, self.limits = 2 * slots + 2, 2 * slots + 3


def split_kernel(operators, *refs):
    high, low, held, ready = refs[-4:]
    live = held.shape[0]

    def copy(k):
        return pltpu.make_async_copy(operators.at[k], held.at[k], ready.at[k])

    for k in range(live):
        copy(k).start()

    def one(k, carry):
        copy(k).wait()
        high[k], low[k] = split(held[k])
        return carry

    lax.fori_loop(0, live, one, 0)


def split_operators(operators, name, earlier=()):
    slots, width, _ = operators.shape
    shape = (slots - 1, width, width)
    return pl.pallas_call(
        split_kernel,
        in_specs=[pl.BlockSpec(memory_space=pltpu.HBM)]
        + [pl.BlockSpec(memory_space=pltpu.VMEM)] * len(earlier),
        out_specs=[pl.BlockSpec(memory_space=pltpu.VMEM)] * 2,
        out_shape=[pltpu.VMEM(shape, BF16)] * 2,
        scratch_shapes=[pltpu.VMEM(shape, F32), pltpu.SemaphoreType.DMA((slots - 1,))],
        compiler_params=pltpu.CompilerParams(vmem_limit_bytes=SPLIT_VMEM_LIMIT),
        cost_estimate=pl.CostEstimate(flops=0, bytes_accessed=operators.size * 4, transcendentals=0),
        name=name,
    )(pltpu.with_memory_space_constraint(operators, pltpu.HBM), *earlier)


def split_blocks(blocks, high, low):
    share = blocks[0].shape[1]
    for place, block in enumerate(blocks):
        rows = pl.ds(place * share, share)
        high[:, rows, :], low[:, rows, :] = split(block[...])


def lanes(value):
    total = jnp.sum(value, axis=tuple(range(value.ndim - 1)))[None]
    width = total.shape[1]
    return sum(total[:, c : c + 128] for c in range(0, width, 128))


def each_live(count, one):
    def three(i, carry):
        one(3 * i, carry)
        one(3 * i + 1, carry)
        return one(3 * i + 2, carry)

    threes = lax.div(count, 3)
    lax.fori_loop(0, threes, three, 0)
    lax.fori_loop(3 * threes, count, one, 0)


def inner_kernel(at, ring, info, *refs):
    blocks = refs[:ring]
    right_high, right_low = refs[ring : ring + 2]
    out_high, out_low, token, high, low = refs[-5:]
    token[...] = jnp.zeros_like(token)
    split_blocks(blocks, high, low)

    def one(k, carry):
        source = info[k]
        out_high[k], out_low[k] = split(
            dot3(high[source], low[source], right_high[k], right_low[k])
        )
        return carry

    each_live(info[at.count], one)


def inner_rows(at, info, blocks, right, earlier=()):
    ring = len(blocks)
    live, width, _ = right[0].shape
    sectors, share, _ = blocks[0].shape
    rows = ring * share
    return call(
        functools.partial(inner_kernel, at, ring),
        "inner_rows",
        info,
        [*blocks, *right, *earlier],
        [((live, rows, width), BF16)] * 2 + [((1, 128), F32)],
        live * rows * width * width * 6,
        [pltpu.VMEM((sectors, rows, width), BF16)] * 2,
    )


def first_row(at, info, ring, share, offset, side):
    around = lax.rem(info[at.ring] + offset, ring)
    return pl.multiple_of((around * 2 + side) * share, share)


def outer_rows(at, info, k, ring, places, left, full, outs):
    share = outs[0].shape[1]
    picks = [pl.ds(first_row(at, info, ring, share, *place), share) for place in places]
    high, low = (
        jnp.concatenate([part[k, pick, :] for pick in picks], axis=0) for part in left
    )
    product = dot3(high, low, full[0][k], full[1][k])
    target = info[at.target + k]
    for i, out in enumerate(outs):
        out[target] += product[i * share : (i + 1) * share]


def middle_kernel(at, ring, lasts, groups, order, head, info, *refs):
    blocks, refs = refs[: len(lasts)], refs[len(lasts) :]
    parts, refs = refs[: 2 * len(groups)], refs[2 * len(groups) :]
    right_high, right_low, left_high, left_low = refs[:4]
    full_high, full_low = refs[4:6]
    outs, (high, low) = refs[6:-2], refs[-2:]
    share = blocks[0].shape[1]
    side = info[at.side]
    split_blocks(blocks, high, low)
    for out in outs:
        out[...] = jnp.zeros_like(out)
    places = [(r, 1 - side) for r in order[: head[0]]] + [(r, side) for r in order[: head[1]]]

    def put(out, k, r, other, value):
        rows = pl.ds(first_row(at, info, ring, share, r, 1 - side if other else side), share)
        out[k, rows, :] = value

    def one(k, carry):
        source = info[k]
        inner = split(dot3(high[source], low[source], right_high[k], right_low[k]))
        for which, out in enumerate((full_high, full_low)):
            for g, group in enumerate(groups):
                for i, (r, other) in enumerate(group):
                    put(out, k, r, other, parts[2 * g + which][k, i * share : (i + 1) * share, :])
            for i, r in enumerate(lasts):
                put(out, k, r, True, inner[which][i * share : (i + 1) * share])
        outer_rows(
            at, info, k, ring, places, (left_high, left_low), (full_high, full_low), outs
        )
        return carry

    each_live(info[at.count], one)


def middle(at, info, ring, lasts, groups, order, head, blocks, parts, right, left):
    live, width, _ = right[0].shape
    sectors, share, _ = blocks[0].shape
    count = sum(head)
    results = call(
        functools.partial(middle_kernel, at, ring, lasts, groups, order, head),
        "middle",
        info,
        [*blocks, *(array for part in parts for array in part), *right, *left],
        [((live, width, width), BF16)] * 2 + [(blocks[0].shape, F32)] * count,
        live * share * (len(lasts) + count) * width * width * 6,
        [pltpu.VMEM((sectors, len(lasts) * share, width), BF16)] * 2,
    )
    return results[:2], results[2 : 2 + head[0]], results[2 + head[0] :]


def outer_kernel(at, ring, wanted, counted, info, *refs):
    full_high, full_low, left_high, left_low = refs[:4]
    outs = refs[-len(wanted) :]
    side = info[at.side]
    for out in outs:
        out[...] = jnp.zeros_like(out)
    places = [(r, 1 - side if other else side) for r, other in wanted]

    def one(k, carry):
        outer_rows(
            at, info, k, ring, places, (left_high, left_low), (full_high, full_low), outs
        )
        return carry

    each_live(info[at.count], one)
    if counted:
        squares, sums = refs[4], refs[-len(wanted) - 1]
        blocks = refs[5 : 5 + 2 * ring]
        totals = [*refs[5 + 2 * ring : 5 + 4 * ring - len(wanted)], *outs]
        dots = sum(lanes(block[...] * total[...]) for block, total in zip(blocks, totals))
        row = lax.broadcasted_iota(jnp.int32, sums.shape, 0)
        sums[...] = jnp.where(row == 0, dots, jnp.where(row == 1, squares[...], 0.0))


def outer_blocks(at, info, ring, wanted, full, left, counted=()):
    live, width, _ = left[0].shape
    share = width // (2 * ring)
    sectors = info.shape[0] - at.limits
    extra = [counted[0], *counted[1], *counted[2]] if counted else []
    return call(
        functools.partial(outer_kernel, at, ring, wanted, bool(counted)),
        "outer_blocks",
        info,
        [*full, *left, *extra],
        ([((8, 128), F32)] if counted else []) + [((sectors, share, width), F32)] * len(wanted),
        0,
    )


def inside(limits, first, start, shape):
    rows = start + lax.broadcasted_iota(jnp.int32, shape[1:], 0)
    cols = lax.broadcasted_iota(jnp.int32, shape[1:], 1)
    return [
        ((rows < limits[first + s]) & (cols < limits[first + s])).astype(F32)
        for s in range(shape[0])
    ]


def begin_kernel(limits, trial, vector, squares):
    total = jnp.zeros(squares.shape, F32)
    start = lax.axis_index("term").astype(jnp.int32) * trial.shape[1]
    for s, mask in enumerate(inside(limits, 0, start, trial.shape)):
        value = mask * trial[s]
        vector[s] = value
        total = total + lanes(value * value)
    squares[...] = total


def begin(limits, trial):
    return call(
        begin_kernel,
        "begin",
        limits,
        [trial],
        [(trial.shape, F32), ((1, 128), F32)],
        trial.size * 4,
    )


def ring_sum(parts):
    parts = [part[...] for part in parts]
    while len(parts) > 1:
        half = len(parts) // 2
        parts = [parts[r] + parts[r + half] for r in range(half)]
    return parts[0]


def finish_kernel(cells, vector, *refs):
    parts, result = refs[:-1], refs[-1]
    total = jnp.sum(ring_sum(parts), axis=1, keepdims=True)
    scale = jnp.sqrt(cells / total)
    for s in range(vector.shape[0]):
        result[s] = vector[s] * scale


def finish(cells, vector, parts):
    return pl.pallas_call(
        functools.partial(finish_kernel, cells),
        in_specs=[pl.BlockSpec(memory_space=pltpu.VMEM)] * (1 + len(parts)),
        out_specs=pl.BlockSpec(memory_space=pltpu.VMEM),
        out_shape=jax.ShapeDtypeStruct(vector.shape, F32),
        compiler_params=pltpu.CompilerParams(vmem_limit_bytes=VMEM_LIMIT),
        name="finish",
    )(vector, *parts)


def update_kernel(at, ring, info, *refs):
    vector, precond, refs = refs[0], refs[1], refs[2:]
    sums, terms, (result, squares, ritz) = refs[:ring], refs[ring:-3], refs[-3:]
    both = jnp.sum(ring_sum(sums), axis=1, keepdims=True)
    theta = both[0:1] / both[1:2]
    ritz[...] = jnp.broadcast_to(theta, ritz.shape)
    total = jnp.zeros(squares.shape, F32)
    start = (info[at.ring] * 2 + info[at.side]) * vector.shape[1]
    for s, mask in enumerate(inside(info, at.limits, start, vector.shape)):
        sig = mask * sum(term[s] for term in terms)
        value = vector[s] - (sig - theta * vector[s]) / precond[s]
        result[s] = value
        total = total + lanes(value * value)
    squares[...] = total


def update(at, info, vector, precond, sums, terms, ring):
    return call(
        functools.partial(update_kernel, at, ring),
        "update",
        info,
        [vector, precond, *sums, *terms],
        [(vector.shape, F32), ((1, 128), F32), ((1, 128), F32)],
        vector.size * 8,
    )


def across(value, terms):
    return lax.ppermute(value, "term", [(i, i ^ 1) for i in range(terms)])


def around(value, terms, shift):
    return lax.ppermute(value, "term", [(i, (i + 2 * shift) % terms) for i in range(terms)])


def stages(sectors, terms):
    inner = [("term", terms, 1)]
    across_sectors = [("sector", sectors, 1 << bit) for bit in range(sectors.bit_length() - 1)]
    outer = [("term", terms, 1 << bit) for bit in range(1, terms.bit_length() - 1)]
    return inner + across_sectors, outer


def stage_sum(values, stage):
    axis, size, step = stage
    return values + lax.ppermute(values, axis, [(i, i ^ step) for i in range(size)])


def send_order(ring):
    ups = ring // 2
    downs = ring - 1 - ups
    order = []
    for hop in range(ups, 0, -1):
        order.append(hop)
        if hop <= downs:
            order.append((ring - hop) % ring)
    return order + [0]


def scatter_sum(own, other, terms, sums, steps):
    ring = terms // 2
    ups = ring // 2
    downs = ring - 1 - ups
    received = {r: across(other[r], terms) for r in send_order(ring)}
    inner, *outer = steps
    sums = stage_sum(sums, inner)
    up = down = None
    for hop in range(ups, 0, -1):
        value = own[hop] + received[hop]
        value, sums = lax.optimization_barrier((value if up is None else value + up, sums))
        up = around(value, terms, 1)
        if hop == ups:
            for stage in outer:
                sums = stage_sum(sums, stage)
        if hop <= downs:
            back = (ring - hop) % ring
            value = own[back] + received[back]
            value, sums = lax.optimization_barrier((value if down is None else value + down, sums))
            down = around(value, terms, -1)
    parts = [sums] + [around(sums, terms, shift) for shift in range(1, ring)]
    return [term for term in (own[0], received[0], up, down) if term is not None], parts


def per_device(
    trial, precond, sector_dims, left_ops, right_ops, task_source, task_target, task_count
):
    sec_dev, share, width = trial.shape
    slots = left_ops.shape[0]
    sectors, terms = lax.axis_size("sector"), lax.axis_size("term")
    ring = terms // 2
    cells = float(sec_dev * sectors * width * width)
    term = lax.axis_index("term").astype(jnp.int32)
    at = Place(slots)
    info = jnp.concatenate(
        [task_source, task_target, jnp.stack([term // 2, term % 2]), task_count, sector_dims]
    )
    values = []
    vector, squares = begin(sector_dims, trial)
    steps, outer_steps = stages(sectors, terms)
    order = send_order(ring)
    ups = ring // 2
    downs = ring - 1 - ups
    last = ring - ups
    head = (ring // 2, ring // 4)
    right = left = None
    for step in range(STEPS):
        mine, theirs, groups, parts = {0: vector}, {}, [], []
        token = None
        for hop in range(1, ups + 1):
            value = mine[(ring - hop + 1) % ring]
            if token is not None:
                value, token = lax.optimization_barrier((value, token))
            mine[ring - hop] = around(value, terms, 1)
            fresh = [(ring - hop + 1) % ring]
            if hop <= downs:
                mine[hop] = around(mine[hop - 1], terms, -1)
            if hop > 1 and hop - 1 <= downs:
                fresh.append(hop - 1)
            for r in fresh:
                theirs[r] = across(mine[r], terms)
            if hop == 1:
                group = [(0, False), (0, True)]
            else:
                group = [(r, False) for r in fresh] + before
            before = [(r, True) for r in fresh]
            if hop == 1:
                before = []
            if right is None:
                right = split_operators(right_ops, "split_right", (theirs[0],))
            *part, token = inner_rows(
                at,
                info,
                [(theirs if other else mine)[r] for r, other in group],
                right,
                () if token is None else (token,),
            )
            groups.append(group)
            parts.append(part)
            if left is None:
                left = split_operators(left_ops, "split_left", (token, mine[1]))
        fresh = [last] + ([ups] if ups <= downs else [])
        for r in fresh:
            theirs[r] = across(mine[r], terms)
        lasts = [r for r, _ in before[1:]] + fresh
        group = [(r, False) for r in fresh] + before[:1]
        *part, token = inner_rows(
            at, info, [(theirs if other else mine)[r] for r, other in group], right, (token,)
        )
        groups.append(group)
        parts.append(part)
        full, others, owns = middle(
            at, info, ring, lasts, groups, order, head, [theirs[r] for r in lasts], parts, right, left
        )
        done = [(r, True) for r in order[: head[0]]] + [(r, False) for r in order[: head[1]]]
        totals = dict(zip(done, [*others, *owns]))
        rest = [(r, True) for r in order[head[0] :]] + [(r, False) for r in order[head[1] :]]
        blocks = [(theirs if other else mine)[r] for r, other in done + rest]
        sums, *outs = outer_blocks(
            at, info, ring, rest, full, left, (squares, blocks, [totals[key] for key in done])
        )
        totals.update(zip(rest, outs))
        owns = {r: totals[r, False] for r in range(ring)}
        others = {r: totals[r, True] for r in range(ring)}
        summed, sums = scatter_sum(owns, others, terms, sums, steps)
        vector, squares, ritz = update(at, info, vector, precond, sums, summed, ring)
        values.append(ritz[0, :1])
    for stage in steps + outer_steps:
        squares = stage_sum(squares, stage)
    return (finish(cells, vector, [squares]), jnp.concatenate(values))


def solution(mesh):
    return jax.shard_map(
        per_device,
        mesh=mesh,
        in_specs=(
            P("sector", "term", None),
            P("sector", "term", None),
            P("sector"),
            P(("sector", "term"), None, None),
            P(("sector", "term"), None, None),
            P(("sector", "term")),
            P(("sector", "term")),
            P(("sector", "term")),
        ),
        out_specs=(P("sector", "term", None), P()),
        check_vma=False,
    )
```
